128 devices in a mesh: grp: 16 (over y, x_lo, core), blk: 8 (over x_hi, z).
Axes of the slice: x: 4 (x_hi: 2, x_lo: 2; x = x_hi * 2 + x_lo), y: 4, z: 4, core: 2. Of those that a mesh axis runs over, the one named last changes fastest.
Arguments:
- queries: bfloat16 [16384, 4096], P(('grp', 'blk')), may hold values from -0.45 to 0.45
- passages: bfloat16 [16384, 4096], P(('grp', 'blk')), may hold values from -0.45 to 0.45
- positives: int32 [16, 1024], P('grp', 'blk'), may hold values from 0 to 1023, as said below
- hard_owner: int32 [16384, 3], P(('grp', 'blk')), may hold values from 0 to 127, all different within a row; in each aligned block of 128 rows (0 to 127, 128 to 255, ...) at most 4 rows name the same one
- hard_row: int32 [16384, 3], P(('grp', 'blk')), may hold values from 0 to 127
Outputs:
- loss: float32 [16384], P(('grp', 'blk'))
- grad_queries: float32 [16384, 4096], P(('grp', 'blk'))
- grad_passages: float32 [16384, 4096], P(('grp', 'blk'))
The draws below stay inside these ranges and needn't reach their ends.
Inputs may be any that keep to these rules, and one draw needn't show every extreme that they name: `hard_owner`: within each aligned block of 128 rows (the queries of one device), no owner is named by more than 4 entries, a bound that some block reaches; the three owners of a row differ. Each row of positives is a permutation of 0 to 1023.
All inputs are finite; a program needn't handle non-finite values.
Results may differ from the reference program's by a relative error of at most 0.013.
Values may be sent and summed in bfloat16 or wider, within the bound.
A program may use at most 128 MiB of HBM per device.

```python
import math
import jax
import jax.numpy as jnp
import numpy as np
from jax import lax

D = 4096
ROWS = 128
NHARD = 3
CAP = 4
GP = 1024
QUERIES = 16384
N_GRP = 16
N_BLK = 8
DEVICES = 128


def passage_table(key):
    base = jnp.clip(0.05 * jax.random.normal(jax.random.fold_in(key, 201), (QUERIES, D), jnp.float32), -0.25, 0.25)
    common = jax.random.uniform(jax.random.fold_in(key, 202), (1, D), jnp.float32, -0.03, 0.03)
    field = base + common
    spread = jnp.clip(0.05 * jax.random.normal(jax.random.fold_in(key, 203), (QUERIES, D), jnp.float32), -0.25, 0.25)
    local = jnp.arange(QUERIES, dtype=jnp.int32) % GP
    partner = local % 64 == 1
    return jnp.where(partner[:, None], jnp.roll(field, 1, axis=0) + 0.6 * spread, field)


def positive_table(key):
    group_keys = jax.random.split(jax.random.fold_in(key, 204), QUERIES // GP)

    def one_group(group_key):
        return jax.random.permutation(group_key, GP)
    return jax.vmap(one_group)(group_keys).astype(jnp.int32)


def draw_positives(key, part):
    table = positive_table(key)
    return table


def draw_passages(key, part):
    field = passage_table(key)
    return field.astype(jnp.bfloat16)


def draw_queries(key, part):
    field = passage_table(key)
    table = positive_table(key).reshape(-1)
    key = jax.random.fold_in(key, 12)
    index = jnp.arange(QUERIES, dtype=jnp.int32)
    target = index // GP * GP + table
    matched = field[target]
    spread = jnp.clip(0.0156 * jax.random.normal(key, (QUERIES, D), jnp.float32), -0.08, 0.08)
    result = 0.0415 * matched + spread
    return result.astype(jnp.bfloat16)


def with_ends(array, rng, least, largest):
    place = [jax.random.randint(jax.random.fold_in(rng, axis), (), 0, length) for axis, length in enumerate(array.shape)]
    longest = array.shape.index(max(array.shape))
    beside = place[:longest] + [(place[longest] + 1) % array.shape[longest]] + place[longest + 1:]
    return array.at[tuple(place)].set(least).at[tuple(beside)].set(largest)


def assign_block(rng, own, number, rows, number_of, top, reach, slope):
    order = jax.random.permutation(rng, number_of)
    crowded, ordinary = shares(number_of, rows * top, reach, slope, True), shares(number_of, rows * top, reach, slope, False)
    places = jnp.arange(number_of)

    def named(lengths, rotation):
        used = int((lengths > 0).sum())
        fixed = max(1, used // 4)
        moved = fixed + (places - fixed + rotation * (used - fixed)) % max(1, number_of - fixed)
        return jnp.zeros((number_of,), jnp.int32).at[order[jnp.where(places < fixed, places, moved)]].set(jnp.asarray(lengths, jnp.int32))

    lengths = jnp.where(number % 4 == 0, named(crowded, number // 4), named(ordinary, number - number // 4 - 1))
    mixed = jax.random.permutation(jax.random.fold_in(own, 3), number_of)
    donor, receiver = mixed[0:number_of // 2 * 2:2], mixed[1:number_of // 2 * 2:2]
    room = jnp.minimum(lengths[donor] - 1, reach - lengths[receiver]) // 2
    room = jnp.where((donor == order[0]) | (receiver == order[0]) | (lengths[receiver] == 0), 0, jnp.maximum(room, 0))
    moved = jax.random.randint(jax.random.fold_in(own, 4), (number_of // 2,), 0, 1 << 20) % (room + 1)
    lengths = lengths.at[donor].add(-moved).at[receiver].add(moved)
    labels = jnp.searchsorted(jnp.cumsum(lengths), jnp.arange(rows * top), side="right").astype(jnp.int32)
    listing = labels.reshape(top, rows).T
    listing = listing[jax.random.permutation(jax.random.fold_in(own, 1), rows)]
    rotation = jax.random.randint(jax.random.fold_in(own, 2), (rows, 1), 0, top)
    return jnp.take_along_axis(listing, (jnp.arange(top)[None, :] + rotation) % top, axis=1)


def shares(number_of, total, reach, skew, full):
    portions = [(1 << 20) // math.isqrt(rank ** skew) + 1 for rank in range(1, number_of + 1)]
    largest = reach if full else min(reach, max(-(-total // number_of), total * portions[0] // sum(portions)))
    least = 1 if total - largest >= number_of - 1 else 0
    given, surplus = [largest] + [least] * (number_of - 1), total - largest - least * (number_of - 1)
    while surplus > 0:
        free = [i for i in range(1, number_of) if given[i] < largest] or [i for i in range(1, number_of) if given[i] < reach]
        pool, remaining = sum([portions[i] for i in free]), surplus
        for i in free:
            extra = min(reach - given[i], max(1, remaining * portions[i] // pool), surplus)
            given[i] = given[i] + extra
            surplus = surplus - extra
    return np.array(given)


def setup_inputs(seed: int = 0) -> dict:
    seeds = jax.random.split(jax.random.key(seed), 6)
    queries = draw_queries(jax.random.fold_in(seeds[5], 71), 0)
    passages = draw_passages(jax.random.fold_in(seeds[5], 71), 0)
    positives = draw_positives(jax.random.fold_in(seeds[5], 71), 0)
    hard_owner_keys = jax.random.split(jax.random.fold_in(seeds[3], 1), QUERIES // ROWS)
    hard_owner_turns = jax.random.permutation(jax.random.fold_in(seeds[3], 3), QUERIES // ROWS)
    hard_owner = jax.vmap(lambda own, number: assign_block(jax.random.fold_in(seeds[3], 2), own, number, ROWS, DEVICES, NHARD, CAP, 2))(hard_owner_keys, hard_owner_turns).reshape((QUERIES, NHARD))
    hard_row = with_ends(jax.random.randint(seeds[4], (QUERIES, NHARD), 0, ROWS), jax.random.fold_in(seeds[4], 1), 0, ROWS - 1).astype(jnp.int32)
    return dict(queries=queries, passages=passages, positives=positives, hard_owner=hard_owner, hard_row=hard_row)


LOGIT_SCALE = 20.0


def group_iteration(hard_total, group, queries, passages, positives, hard_id):
    start = group * GP
    qg = lax.dynamic_slice_in_dim(queries, start, GP, 0)
    pg = lax.dynamic_slice_in_dim(passages, start, GP, 0)
    pos = lax.dynamic_index_in_dim(positives, group, 0, keepdims=False)
    ids = lax.dynamic_slice_in_dim(hard_id, start, GP, 0)
    scores = jnp.dot(qg, pg.T, preferred_element_type=jnp.float32) * LOGIT_SCALE
    hard = passages[ids]
    hard_shift = math.log(GP / NHARD)
    hard_scores = jnp.einsum('qd,qkd->qk', qg.astype(jnp.float32), hard.astype(jnp.float32)) * LOGIT_SCALE + hard_shift
    top = jnp.maximum(jnp.max(scores, axis=1), jnp.max(hard_scores, axis=1))
    total = jnp.sum(jnp.exp(scores - top[:, None]), axis=1) + jnp.sum(jnp.exp(hard_scores - top[:, None]), axis=1)
    lse = top + jnp.log(total)
    columns = jnp.arange(GP, dtype=jnp.int32)
    indicator_vector = (columns[None, :] == pos[:, None]).astype(jnp.float32)
    spos = jnp.sum(scores * indicator_vector, axis=1)
    loss = lse - spos
    coef = (jnp.exp(scores - lse[:, None]) - indicator_vector).astype(jnp.bfloat16)
    hard_coef = jnp.exp(hard_scores - lse[:, None])
    query_gradient = LOGIT_SCALE * jnp.einsum('qk,qkd->qd', hard_coef, hard.astype(jnp.float32))
    grad_p = jnp.zeros((GP, D), jnp.float32)
    for block in range(N_BLK):
        lo = block * ROWS
        part_q = jnp.dot(coef[:, lo:lo + ROWS], pg[lo:lo + ROWS], preferred_element_type=jnp.float32) * LOGIT_SCALE
        query_gradient = query_gradient + part_q.astype(jnp.bfloat16).astype(jnp.float32)
        part_p = jnp.dot(coef[lo:lo + ROWS].T, qg[lo:lo + ROWS], preferred_element_type=jnp.float32) * LOGIT_SCALE
        grad_p = grad_p + part_p.astype(jnp.bfloat16).astype(jnp.float32)
    hard_part = (LOGIT_SCALE * hard_coef[:, :, None] * qg.astype(jnp.float32)[:, None, :]).astype(jnp.bfloat16)
    hard_total = hard_total.at[ids.reshape(-1)].add(hard_part.reshape(-1, D).astype(jnp.float32))
    return hard_total, (loss, query_gradient, grad_p)


def reference(queries, passages, positives, hard_owner, hard_row):
    hard_id = (hard_owner * ROWS + hard_row).astype(jnp.int32)

    def step(carry, group):
        return group_iteration(carry, group, queries, passages, positives, hard_id)

    initial_total = jnp.zeros((QUERIES, D), jnp.float32)
    hard_total, (loss, query_gradient, grad_p) = lax.scan(step, initial_total, jnp.arange(N_GRP, dtype=jnp.int32))
    grad_passages = grad_p.reshape(QUERIES, D) + hard_total
    return loss.reshape(QUERIES), query_gradient.reshape(QUERIES, D), grad_passages
```

```python
import functools
import math

import jax
import jax.numpy as jnp
from jax import lax
from jax.experimental import pallas as pl
from jax.experimental.pallas import tpu as pltpu
from jax.sharding import PartitionSpec as P

LOGIT_SCALE = 20.0
ROWS = 128
CAP = 4
NCH = 4
NEG = -1e30
MESH = pl.DeviceIdType.MESH
F32 = jnp.float32
BF16 = jnp.bfloat16


def iota(shape, dim):
    return lax.broadcasted_iota(jnp.int32, shape, dim)


def to_column(row):
    n = row.shape[1]
    eye = iota((n, n), 0) == iota((n, n), 1)
    return jnp.sum(jnp.where(eye, row, jnp.zeros_like(row)), axis=1, keepdims=True)


def to_row(col):
    n = col.shape[0]
    eye = iota((n, n), 0) == iota((n, n), 1)
    return jnp.sum(jnp.where(eye, col, jnp.zeros_like(col)), axis=0, keepdims=True)


def mm(a, b):
    return jnp.dot(a, b, preferred_element_type=F32)


def mm_t(a, b):
    return lax.dot_general(a, b, (((1,), (1,)), ((), ())), preferred_element_type=F32)


def kernel(
    NY, NC, D, shift,
    q_hbm, p_hbm, pos_ref, own_ref, row_ref,
    loss_ref, gq_ref, gp_ref,
    PZ, QX, SP, SQ, RP, RQ,
    rs_a, rs_up, rs_dn, rr_a, rr_up, rr_dn, gx_s, gx_r,
    s_own, s_par, hs, gather, coef_o, coef_p, coef_t, hmat,
    xt_s, xt_r, w_s, w_r, j_s, j_r, cx_s, cx_r, c_s, c_r, st_s, st_r, lse_s, lse_r,
    in_sem, ag_send, ag_recv, hard_send, hard_recv,
    xt_send, xt_recv, cx_send, cx_recv, small_send, small_recv, pair_send, pair_recv, rs_send, rs_recv,
):
    R = 4 * NY * NC
    S = 16 * R
    DC = D // NCH
    H = DC // 2
    HD = D // 2
    TN = min(512, H)
    g = lax.axis_index("grp")
    b = lax.axis_index("blk")
    z = lax.rem(b, 4)
    xh = b // 4
    c = lax.rem(g, NC)
    x = xh * 2 + lax.rem(g // NC, 2)
    y = g // (2 * NC)

    def dev(dx, dy, dz, dc):
        x2 = lax.rem(x + dx, 4)
        y2 = lax.rem(y + dy, NY)
        z2 = lax.rem(z + dz, 4)
        c2 = lax.rem(c + dc, NC)
        return ((y2 * 2 + lax.rem(x2, 2)) * NC + c2, (x2 // 2) * 4 + z2)

    def order(n):
        cc = lax.rem(n, NC)
        i = lax.rem(n // NC, 4)
        s = n // (4 * NC)
        a = lax.rem(1 + 2 * i + i // 2, 4)
        yy = lax.rem(a + s + 1, NY)
        return a, yy, cc, (a * NY + yy) * NC + cc

    p_in = pltpu.make_async_copy(p_hbm, PZ.at[pl.ds(z * ROWS, ROWS)], in_sem.at[0])
    q_in = pltpu.make_async_copy(q_hbm, QX.at[pl.ds(x * ROWS, ROWS)], in_sem.at[1])
    p_in.start()
    q_in.start()
    barrier = pltpu.get_barrier_semaphore()

    def greet(n, carry):
        a, yy, cc, r = order(n)

        @pl.when(r > 0)
        def _():
            pl.semaphore_signal(barrier, inc=1, device_id=dev(a, yy, 0, cc), device_id_type=MESH)

        @pl.when(a > 0)
        def _():
            pl.semaphore_signal(barrier, inc=1, device_id=dev(0, yy, a, cc), device_id_type=MESH)

        return carry

    lax.fori_loop(0, R, greet, 0)
    pl.semaphore_wait(barrier, (R - 1) + 3 * NY * NC)
    p_in.wait()
    q_in.wait()

    def block(buf, i, col, width):
        return buf.at[pl.ds(lax.rem(i + 4, 4) * ROWS, ROWS), pl.ds(col, width)]

    def ring(which, kind, ch):
        buf, me = ((PZ, z), (QX, x))[which]
        step = 1 if kind in (0, 2) else 3
        blk = me if kind < 2 else (me - 1 if kind == 2 else me + 1)
        col = ch * DC + (H if kind == 3 else 0)
        width = DC if kind < 2 else H
        ref = block(buf, blk, col, width)
        target = dev(0, 0, step, 0) if which == 0 else dev(step, 0, 0, 0)
        return pltpu.make_async_remote_copy(
            ref, ref, ag_send.at[which, kind, ch], ag_recv.at[which, kind, ch],
            device_id=target, device_id_type=MESH,
        )

    def arriving(which, kind, ch):
        buf, me = ((PZ, z), (QX, x))[which]
        blk = (me - 1, me + 1, me - 2, me + 2)[kind]
        col = ch * DC + (H if kind == 3 else 0)
        width = DC if kind < 2 else H
        ref = block(buf, blk, col, width)
        return pltpu.make_async_remote_copy(
            ref, ref, ag_send.at[which, kind, ch], ag_recv.at[which, kind, ch],
            device_id=dev(0, 0, 1, 0), device_id_type=MESH,
        )

    def own_sends(ch):
        for which in (0, 1):
            ring(which, 0, ch).start()
            ring(which, 1, ch).start()

    own_sends(0)
    own_sends(1)

    lane = iota((1, S), 1)
    slot_r = lane // 16
    slot_b = lax.rem(lane, 16) // 4
    slot_t = lax.rem(lane, 4)
    r_a = slot_r // (NY * NC)
    r_y = lax.rem(slot_r // NC, NY)
    r_c = lax.rem(slot_r, NC)

    def dev_id(x2, y2, z2, c2):
        return ((y2 * 2 + lax.rem(x2, 2)) * NC + c2) * 8 + (x2 // 2) * 4 + z2

    owner = own_ref[...]
    hrow = row_ref[...].astype(F32)
    ndev = 8 * 2 * NY * NC
    width = max(ndev, 128)
    lane_o = iota((ROWS, width), 1)
    hot = [(owner[:, k : k + 1] == lane_o).astype(F32) for k in range(3)]
    count = hot[0] + hot[1] + hot[2]
    lower = (iota((ROWS, ROWS), 1) < iota((ROWS, ROWS), 0)).astype(BF16)
    before = mm(lower, count.astype(BF16))
    rank = [jnp.sum(h * before, axis=1, keepdims=True).astype(jnp.int32) for h in hot]

    def code(k):
        return owner[:, k : k + 1] * CAP + rank[k]

    codes = [jnp.where(owner[:, k : k + 1] >= 0, code(k), -1) for k in range(3)]
    codes_p = (
        dev_id(lax.rem(x + 4 - r_a, 4), lax.rem(y + NY - r_y, NY), slot_b, lax.rem(c + NC - r_c, NC)) * CAP + slot_t
    )

    def codes_q(dx):
        full = dev_id(lax.rem(x + dx, 4), lax.rem(y + r_y, NY), lax.rem(z + r_a, 4), lax.rem(c + r_c, NC)) * CAP + slot_t
        return jnp.where(slot_b == x, full, -2)

    def pick(code_row, values):
        total = jnp.zeros((ROWS, S), F32)
        for k in range(3):
            total = total + jnp.where(codes[k] == code_row, values[k], 0.0)
        return jnp.sum(total, axis=0, keepdims=True)

    rows_k = [hrow[:, k : k + 1] for k in range(3)]
    w_row = pick(codes_p, rows_k)
    w_s[0] = w_row
    w_r[0] = w_row

    def spread(kind, src, dst, wide):
        def body(n, carry):
            a, yy, cc, r = order(n)

            @pl.when(r > 0)
            def _():
                neg = (lax.rem(4 - a, 4), lax.rem(NY - yy, NY), lax.rem(NC - cc, NC))
                target = dev(neg[0], neg[1], 0, neg[2]) if kind == 0 else dev(0, yy, a, cc)
                pltpu.make_async_remote_copy(
                    src.at[0], dst.at[r], small_send.at[wide], small_recv.at[wide],
                    device_id=target, device_id_type=MESH,
                ).start()

            return carry

        lax.fori_loop(0, R, body, 0)

    def spread_all(dst, wide):
        return pltpu.make_async_remote_copy(
            dst.at[pl.ds(1, R - 1)], dst.at[pl.ds(1, R - 1)], small_send.at[wide], small_recv.at[wide],
            device_id=dev(1, 0, 0, 0), device_id_type=MESH,
        )

    def fold(ref):
        values = ref[...]
        keep = iota((R, 1, S), 2) // 16 == iota((R, 1, S), 0)
        return jnp.sum(jnp.where(keep, values, 0.0), axis=0)

    spread(0, w_s, w_r, 0)

    query_number = iota((ROWS, 1), 0).astype(F32)
    pos_row = pos_ref[...].astype(F32)
    pos_wide = jnp.concatenate([pos_row] + [jnp.zeros((1, S - ROWS), F32)], axis=1)
    sub8 = iota((8, S), 0)
    for dx in range(4):
        cq = codes_q(dx)
        v_row = pick(cq, [query_number] * 3)
        jj_row = pick(cq, rows_k)
        table = jnp.where(sub8 == 0, v_row, 0.0) + jnp.where(sub8 == 1, jj_row, 0.0) + jnp.where(sub8 == 2, pos_wide, 0.0)
        xt_s[dx] = table
        if dx == 0:
            xt_r[0] = table

    def x_peer(src, dst, send, recv, dx):
        return pltpu.make_async_remote_copy(
            src.at[dx], dst.at[dx], send.at[dx], recv.at[dx], device_id=dev(dx, 0, 0, 0), device_id_type=MESH
        )

    for dx in range(1, 4):
        x_peer(xt_s, xt_r, xt_send, xt_recv, dx).start()
    for dx in range(1, 4):
        x_peer(xt_s, xt_r, xt_send, xt_recv, dx).wait_recv()
    tables = xt_r[0] + xt_r[1] + xt_r[2] + xt_r[3]
    v_all = tables[0:1, :]
    j_s[0] = tables[1:2, :]
    j_r[0] = tables[1:2, :]
    spread(1, j_s, j_r, 1)

    def gather_matrix(index, slot):
        n = iota((S, 1), 0)
        want = to_column(index).astype(jnp.int32) + lax.rem(n, 16) // 4 * ROWS
        gather[slot] = (want == iota((S, 4 * ROWS), 1)).astype(BF16)

    spread_all(w_r, 0).wait_recv()
    gather_matrix(fold(w_r), 0)
    gather_matrix(v_all, 1)

    def hard_starts(kind, ch):
        src, dst = ((SP, RP), (SQ, RQ))[kind]

        def body(n, carry):
            a, yy, cc, r = order(n)

            @pl.when(r > 0)
            def _():
                target = dev(a, yy, 0, cc) if kind == 0 else dev(0, yy, a, cc)
                pltpu.make_async_remote_copy(
                    src.at[pl.ds(r * 16, 16), pl.ds(ch * DC, DC)], dst.at[pl.ds(r * 16, 16), pl.ds(ch * DC, DC)],
                    hard_send.at[kind, ch], hard_recv.at[kind, ch], device_id=target, device_id_type=MESH,
                ).start()

            return carry

        lax.fori_loop(0, R, body, 0)

    def hard_all(kind, ch):
        src, dst = ((SP, RP), (SQ, RQ))[kind]
        ref = lambda buf: buf.at[pl.ds(16, S - 16), pl.ds(ch * DC, DC)]
        return pltpu.make_async_remote_copy(
            ref(src), ref(dst), hard_send.at[kind, ch], hard_recv.at[kind, ch],
            device_id=dev(1, 0, 0, 0), device_id_type=MESH,
        )

    def tiles(start, length, body):
        def step(t, carry):
            body(pl.ds(pl.multiple_of(start + t * TN, 128), TN))
            return carry

        lax.fori_loop(0, length // TN, step, 0)

    def serve(kind, ch):
        src, out, mine = ((PZ, SP, RP), (QX, SQ, RQ))[kind]

        def body(cols):
            rows = mm(gather[kind], src[:, cols]).astype(BF16)
            out[:, cols] = rows
            mine[0:16, cols] = rows[0:16]

        tiles(ch * DC, DC, body)

    me_rows = pl.ds(x * ROWS, ROWS)
    par_rows = pl.ds(lax.rem(x + 2, 4) * ROWS, ROWS)
    s_own[...] = jnp.zeros_like(s_own)
    s_par[...] = jnp.zeros_like(s_par)
    hs[...] = jnp.zeros_like(hs)

    def score(acc, rows, keys, ch):
        def body(cols):
            acc[...] += mm_t(QX[rows, cols], keys[:, cols])

        tiles(ch * DC, DC, body)

    for ch in range(NCH):
        for which in (0, 1):
            for kind in (0, 1):
                arriving(which, kind, ch).wait_recv()
                ring(which, kind + 2, ch).start()
        if ch + 2 < NCH:
            own_sends(ch + 2)
        arriving(0, 2, ch).wait_recv()
        arriving(0, 3, ch).wait_recv()
        serve(0, ch)
        hard_starts(0, ch)
        score(s_own, me_rows, PZ, ch)
    for ch in range(NCH):
        arriving(1, 2, ch).wait_recv()
        arriving(1, 3, ch).wait_recv()
        serve(1, ch)
        hard_starts(1, ch)
    for ch in range(NCH):
        score(s_par, par_rows, PZ, ch)

    base = (xh * 4 * ROWS).astype(F32)
    lane_p = iota((ROWS, 4 * ROWS), 1).astype(F32)
    pos_own = to_column(pos_row) - base
    pos_par = to_column(xt_r[2][2:3, 0:ROWS]) - base

    def half_stats(acc, pos):
        s = acc[...] * LOGIT_SCALE
        m = jnp.max(s, axis=1, keepdims=True)
        l = jnp.sum(jnp.exp(s - m), axis=1, keepdims=True)
        sp = jnp.sum(jnp.where(lane_p == pos, s, 0.0), axis=1, keepdims=True)
        return m, l, sp

    lane128 = iota((ROWS, 128), 1)
    m_p, l_p, sp_p = half_stats(s_par, pos_par)
    st_s[...] = jnp.where(lane128 == 0, m_p, jnp.where(lane128 == 1, l_p, jnp.where(lane128 == 2, sp_p, 0.0)))

    def pair(src, dst, i):
        return pltpu.make_async_remote_copy(
            src, dst, pair_send.at[i], pair_recv.at[i], device_id=dev(2, 0, 0, 0), device_id_type=MESH
        )

    pair(st_s, st_r, 0).start()
    m_o, l_o, sp_o = half_stats(s_own, pos_own)

    for ch in range(NCH):
        hard_all(0, ch).wait_recv()
        score(hs, me_rows, RP, ch)
    pair(st_s, st_r, 0).wait_recv()
    stats = st_r[...]
    m_r, l_r, sp_r = stats[:, 0:1], stats[:, 1:2], stats[:, 2:3]
    scaled = hs[...] * LOGIT_SCALE + shift
    mask = [codes[k] == codes_p for k in range(3)]
    hard_k = [jnp.sum(jnp.where(mask[k], scaled, 0.0), axis=1, keepdims=True) for k in range(3)]
    present = [jnp.where(owner[:, k : k + 1] >= 0, hard_k[k], NEG) for k in range(3)]
    top = jnp.maximum(jnp.maximum(m_o, m_r), jnp.maximum(jnp.maximum(present[0], present[1]), present[2]))
    total = l_o * jnp.exp(m_o - top) + l_r * jnp.exp(m_r - top)
    for k in range(3):
        total = total + jnp.exp(present[k] - top)
    lse = top + jnp.log(total)
    lse_s[...] = jnp.broadcast_to(lse, (ROWS, 128))
    pair(lse_s, lse_r, 1).start()
    loss_ref[...] = to_row(lse - (sp_o + sp_r))
    hard_coef = [jnp.exp(present[k] - lse) for k in range(3)]

    for dx in range(4):
        row = pick(codes_q(dx), hard_coef)
        cx_s[dx] = row
        if dx == 0:
            cx_r[0] = row
    for dx in range(1, 4):
        x_peer(cx_s, cx_r, cx_send, cx_recv, dx).start()

    def half_coef(acc, pos, row_lse, out, column):
        f = jnp.exp(acc[...] * LOGIT_SCALE - row_lse) - jnp.where(lane_p == pos, 1.0, 0.0)
        out[...] = f.astype(BF16)
        coef_t[:, column * ROWS : (column + 1) * ROWS] = jnp.transpose(f).astype(BF16)

    half_coef(s_own, pos_own, lse, coef_o, 0)
    pair(lse_s, lse_r, 1).wait_recv()
    half_coef(s_par, pos_par, lse_r[:, 0:1], coef_p, 1)

    def passage_part(offset, cols):
        ct = coef_t[pl.ds(lax.rem(z + offset, 4) * ROWS, ROWS), :]
        part = mm(ct[:, 0:ROWS], QX[me_rows, cols]) + mm(ct[:, ROWS : 2 * ROWS], QX[par_rows, cols])
        return part * LOGIT_SCALE

    def rs(src, dst, i, step, start, length):
        return pltpu.make_async_remote_copy(
            src.at[:, pl.ds(start, length)], dst.at[:, pl.ds(start, length)], rs_send.at[i], rs_recv.at[i],
            device_id=dev(0, 0, step, 0), device_id_type=MESH,
        )

    far_up = rs(rs_a, rr_a, 0, 1, 0, HD)
    far_dn = rs(rs_a, rr_a, 1, 3, HD, HD)
    up_free = rs(rs_up, rr_up, 2, 1, HD, HD)
    dn_free = rs(rs_dn, rr_dn, 3, 3, 0, HD)
    up_last = rs(rs_up, rr_up, 4, 1, 0, HD)
    dn_last = rs(rs_dn, rr_dn, 5, 3, HD, HD)

    def far(cols):
        rs_a[:, cols] = passage_part(2, cols).astype(BF16)

    tiles(0, HD, far)
    far_up.start()
    tiles(HD, HD, far)
    far_dn.start()

    def partner_part(cols):
        gx_s[:, cols] = (mm(coef_p[...], PZ[:, cols]) * LOGIT_SCALE).astype(BF16)

    tiles(0, D, partner_part)
    pair(gx_s, gx_r, 2).start()

    def up_part(cols):
        rs_up[:, cols] = passage_part(1, cols).astype(BF16)

    def dn_part(cols):
        rs_dn[:, cols] = passage_part(3, cols).astype(BF16)

    tiles(HD, HD, up_part)
    up_free.start()
    tiles(0, HD, dn_part)
    dn_free.start()

    for dx in range(1, 4):
        x_peer(cx_s, cx_r, cx_send, cx_recv, dx).wait_recv()
    c_row = cx_r[0] + cx_r[1] + cx_r[2] + cx_r[3]
    c_s[0] = c_row
    c_r[0] = c_row
    spread(1, c_s, c_r, 2)

    far_up.wait_recv()

    def up_sum(cols):
        rs_up[:, cols] = (passage_part(1, cols) + rr_a[:, cols].astype(F32)).astype(BF16)

    tiles(0, HD, up_sum)
    up_last.start()
    far_dn.wait_recv()

    def dn_sum(cols):
        rs_dn[:, cols] = (passage_part(3, cols) + rr_a[:, cols].astype(F32)).astype(BF16)

    tiles(HD, HD, dn_sum)
    dn_last.start()

    h = jnp.zeros((ROWS, S), F32)
    for k in range(3):
        h = h + jnp.where(mask[k], hard_coef[k], 0.0)
    hmat[...] = h.astype(BF16)
    pair(gx_s, gx_r, 2).wait_recv()

    def query_grad(cols):
        part = mm(coef_o[...], PZ[:, cols]) + mm(hmat[...], RP[:, cols])
        gq_ref[:, cols] = part * LOGIT_SCALE + gx_r[:, cols].astype(F32)

    tiles(0, D, query_grad)

    spread_all(j_r, 1).wait_recv()
    spread_all(c_r, 2).wait_recv()
    j_row = fold(j_r).astype(jnp.int32)
    hmat[...] = jnp.where(iota((ROWS, S), 0) == j_row, fold(c_r), 0.0).astype(BF16)
    for ch in range(NCH):
        hard_all(1, ch).wait_recv()

        def passage_grad(cols):
            gp_ref[:, cols] = passage_part(0, cols) + LOGIT_SCALE * mm(hmat[...], RQ[:, cols])

        tiles(ch * DC, DC, passage_grad)
    up_free.wait_recv()
    dn_free.wait_recv()
    up_last.wait_recv()
    dn_last.wait_recv()

    def last(cols):
        gp_ref[:, cols] += rr_up[:, cols].astype(F32) + rr_dn[:, cols].astype(F32)

    tiles(0, D, last)

    for ch in range(NCH):
        for which in (0, 1):
            for kind in range(4):
                ring(which, kind, ch).wait_send()
            hard_all(which, ch).wait_send()
    for dx in range(1, 4):
        x_peer(xt_s, xt_r, xt_send, xt_recv, dx).wait_send()
        x_peer(cx_s, cx_r, cx_send, cx_recv, dx).wait_send()
    spread_all(w_r, 0).wait_send()
    spread_all(j_r, 1).wait_send()
    spread_all(c_r, 2).wait_send()
    pair(st_s, st_r, 0).wait_send()
    pair(lse_s, lse_r, 1).wait_send()
    pair(gx_s, gx_r, 2).wait_send()
    for copy in (far_up, far_dn, up_free, dn_free, up_last, dn_last):
        copy.wait_send()


def on_device(ngrp, queries, passages, positives, hard_owner, hard_row):
    D = queries.shape[1]
    NC = 2 if ngrp % 4 == 0 else 1
    NY = ngrp // (2 * NC)
    R = 4 * NY * NC
    S = 16 * R
    shift = math.log(8 * ROWS / 3)
    vmem = pltpu.VMEM
    dma = pltpu.SemaphoreType.DMA
    wide = vmem((ROWS, D), BF16)
    any_spec = pl.BlockSpec(memory_space=pl.ANY)
    vmem_spec = pl.BlockSpec(memory_space=pltpu.VMEM)
    loss, gq, gp = pl.pallas_call(
        functools.partial(kernel, NY, NC, D, shift),
        out_shape=(
            jax.ShapeDtypeStruct((1, ROWS), F32),
            jax.ShapeDtypeStruct((ROWS, D), F32),
            jax.ShapeDtypeStruct((ROWS, D), F32),
        ),
        in_specs=[any_spec, any_spec, vmem_spec, vmem_spec, vmem_spec],
        out_specs=(vmem_spec,) * 3,
        scratch_shapes=[
            vmem((4 * ROWS, D), BF16), vmem((4 * ROWS, D), BF16),
            vmem((S, D), BF16), vmem((S, D), BF16), vmem((S, D), BF16), vmem((S, D), BF16),
            wide, wide, wide, wide, wide, wide, wide, wide,
            vmem((ROWS, 4 * ROWS), F32), vmem((ROWS, 4 * ROWS), F32), vmem((ROWS, S), F32),
            vmem((2, S, 4 * ROWS), BF16),
            vmem((ROWS, 4 * ROWS), BF16), vmem((ROWS, 4 * ROWS), BF16), vmem((4 * ROWS, 2 * ROWS), BF16),
            vmem((ROWS, S), BF16),
            vmem((4, 8, S), F32), vmem((4, 8, S), F32),
            vmem((1, 1, S), F32), vmem((R, 1, S), F32),
            vmem((1, 1, S), F32), vmem((R, 1, S), F32),
            vmem((4, 1, S), F32), vmem((4, 1, S), F32),
            vmem((1, 1, S), F32), vmem((R, 1, S), F32),
            vmem((ROWS, 128), F32), vmem((ROWS, 128), F32), vmem((ROWS, 128), F32), vmem((ROWS, 128), F32),
            dma((2,)), dma((2, 4, NCH)), dma((2, 4, NCH)), dma((2, NCH)), dma((2, NCH)),
            dma((4,)), dma((4,)), dma((4,)), dma((4,)), dma((3,)), dma((3,)), dma((3,)), dma((3,)),
            dma((6,)), dma((6,)),
        ],
        compiler_params=pltpu.CompilerParams(
            collective_id=0, has_side_effects=True, vmem_limit_bytes=60 * 2**20
        ),
        cost_estimate=pl.CostEstimate(flops=9 * 10**9, bytes_accessed=8 * 2**20, transcendentals=2 * 10**5),
        name="infonce",
    )(queries, passages, positives, hard_owner, hard_row)
    return loss.reshape(ROWS), gq, gp


def solution(mesh):
    return jax.shard_map(
        functools.partial(on_device, mesh.shape["grp"]),
        mesh=mesh,
        in_specs=(
            P(("grp", "blk"), None),
            P(("grp", "blk"), None),
            P("grp", "blk"),
            P(("grp", "blk"), None),
            P(("grp", "blk"), None),
        ),
        out_specs=(P(("grp", "blk")), P(("grp", "blk"), None), P(("grp", "blk"), None)),
        check_vma=False,
    )
```

```python
import functools
import math

import jax
import jax.numpy as jnp
from jax import lax
from jax.experimental import pallas as pl
from jax.experimental.pallas import tpu as pltpu
from jax.sharding import PartitionSpec as P

LOGIT_SCALE = 20.0
ROWS = 128
CAP = 4
NCH = 4
NEG = -1e30
MESH = pl.DeviceIdType.MESH
F32 = jnp.float32
BF16 = jnp.bfloat16


def iota(shape, dim):
    return lax.broadcasted_iota(jnp.int32, shape, dim)


def to_column(row):
    n = row.shape[1]
    eye = iota((n, n), 0) == iota((n, n), 1)
    return jnp.sum(jnp.where(eye, row, jnp.zeros_like(row)), axis=1, keepdims=True)


def to_row(col):
    n = col.shape[0]
    eye = iota((n, n), 0) == iota((n, n), 1)
    return jnp.sum(jnp.where(eye, col, jnp.zeros_like(col)), axis=0, keepdims=True)


def mm(a, b):
    return jnp.dot(a, b, preferred_element_type=F32)


def mm_t(a, b):
    return lax.dot_general(a, b, (((1,), (1,)), ((), ())), preferred_element_type=F32)


def kernel(
    NY, NC, D, shift,
    q_hbm, p_hbm, pos_ref, own_ref, row_ref,
    loss_ref, gq_hbm, gp_hbm,
    PZ, QX, SP, SQ, RP, RQ,
    rs_a, rs_up, rs_dn, rr_a, rr_up, rr_dn, gx_s, gx_r,
    s_own, s_par, hs, gather, coef_o, coef_p, coef_t, hmat,
    xt_s, xt_r, w_s, w_r, cx_s, cx_r, c_s, c_r, st_s, st_r, lse_s, lse_r, gq_ref, gp_ref,
    in_sem, out_sem, ag_send, ag_recv, hard_send, hard_recv,
    xt_send, xt_recv, cx_send, cx_recv, small_send, small_recv, pair_send, pair_recv, rs_send, rs_recv,
):
    R = 4 * NY * NC
    S = 16 * R
    DC = D // NCH
    H = DC // 2
    HD = D // 2
    TN = min(512, H)
    g = lax.axis_index("grp")
    b = lax.axis_index("blk")
    z = lax.rem(b, 4)
    xh = b // 4
    c = lax.rem(g, NC)
    x = xh * 2 + lax.rem(g // NC, 2)
    y = g // (2 * NC)

    def dev(dx, dy, dz, dc):
        x2 = lax.rem(x + dx, 4)
        y2 = lax.rem(y + dy, NY)
        z2 = lax.rem(z + dz, 4)
        c2 = lax.rem(c + dc, NC)
        return ((y2 * 2 + lax.rem(x2, 2)) * NC + c2, (x2 // 2) * 4 + z2)

    def order(n):
        cc = lax.rem(n, NC)
        i = lax.rem(n // NC, 4)
        s = n // (4 * NC)
        a = lax.rem(1 + 2 * i + i // 2, 4)
        yy = lax.rem(a + s + 1, NY)
        return a, yy, cc, (a * NY + yy) * NC + cc

    p_in = pltpu.make_async_copy(p_hbm, PZ.at[pl.ds(z * ROWS, ROWS)], in_sem.at[0])
    q_in = pltpu.make_async_copy(q_hbm, QX.at[pl.ds(x * ROWS, ROWS)], in_sem.at[1])
    p_in.start()
    q_in.start()
    barrier = pltpu.get_barrier_semaphore()

    def greet(n, carry):
        a, yy, cc, r = order(n)

        @pl.when(r > 0)
        def _():
            pl.semaphore_signal(barrier, inc=1, device_id=dev(a, yy, 0, cc), device_id_type=MESH)

        @pl.when(a > 0)
        def _():
            pl.semaphore_signal(barrier, inc=1, device_id=dev(0, yy, a, cc), device_id_type=MESH)

        return carry

    lax.fori_loop(0, R, greet, 0)
    lane = iota((1, S), 1)
    slot_r = lane // 16
    slot_b = lax.rem(lane, 16) // 4
    slot_t = lax.rem(lane, 4)
    r_a = slot_r // (NY * NC)
    r_y = lax.rem(slot_r // NC, NY)
    r_c = lax.rem(slot_r, NC)

    def dev_id(x2, y2, z2, c2):
        return ((y2 * 2 + lax.rem(x2, 2)) * NC + c2) * 8 + (x2 // 2) * 4 + z2

    owner = [to_column(own_ref[k : k + 1, :].astype(F32)) for k in range(3)]
    hrow = [to_column(row_ref[k : k + 1, :].astype(F32)) for k in range(3)]
    ndev = 8 * 2 * NY * NC
    lane_o = iota((ROWS, max(ndev, 128)), 1).astype(F32)
    hot = [(owner[k] == lane_o).astype(F32) for k in range(3)]
    count = hot[0] + hot[1] + hot[2]
    lower = (iota((ROWS, ROWS), 1) < iota((ROWS, ROWS), 0)).astype(BF16)
    before = mm(lower, count.astype(BF16))
    rank = [jnp.sum(h * before, axis=1, keepdims=True) for h in hot]
    codes = [jnp.where(owner[k] >= 0, owner[k] * CAP + rank[k], -1.0) for k in range(3)]
    codes_p = (
        dev_id(lax.rem(x + 4 - r_a, 4), lax.rem(y + NY - r_y, NY), slot_b, lax.rem(c + NC - r_c, NC)) * CAP + slot_t
    ).astype(F32)

    def codes_q(dx):
        full = dev_id(lax.rem(x + dx, 4), lax.rem(y + r_y, NY), lax.rem(z + r_a, 4), lax.rem(c + r_c, NC)) * CAP + slot_t
        return jnp.where(slot_b == x, full, -2).astype(F32)

    def pick(code_row, values):
        total = jnp.zeros((ROWS, S), F32)
        for k in range(3):
            total = total + jnp.where(codes[k] == code_row, values[k], 0.0)
        return jnp.sum(total, axis=0, keepdims=True)

    w_row = pick(codes_p, hrow)
    w_s[0] = w_row
    w_r[0] = w_row
    query_number = iota((ROWS, 1), 0).astype(F32)
    query_and_row = [query_number + ROWS * hrow[k] for k in range(3)]
    pos_row = pos_ref[...].astype(F32)
    pos_wide = jnp.concatenate([pos_row] + [jnp.zeros((1, S - ROWS), F32)], axis=1)
    for dx in range(4):
        table = jnp.where(iota((2, S), 0) == 0, pick(codes_q(dx), query_and_row), pos_wide)
        xt_s[dx] = table
        if dx == 0:
            xt_r[0] = table

    pl.semaphore_wait(barrier, (R - 1) + 3 * NY * NC)
    p_in.wait()
    q_in.wait()

    def block(buf, i, col, width):
        return buf.at[pl.ds(lax.rem(i + 4, 4) * ROWS, ROWS), pl.ds(col, width)]

    def ring(which, kind, ch):
        buf, me = ((PZ, z), (QX, x))[which]
        step = 1 if kind in (0, 2) else 3
        blk = me if kind < 2 else (me - 1 if kind == 2 else me + 1)
        col = ch * DC + (H if kind == 3 else 0)
        width = DC if kind < 2 else H
        ref = block(buf, blk, col, width)
        target = dev(0, 0, step, 0) if which == 0 else dev(step, 0, 0, 0)
        return pltpu.make_async_remote_copy(
            ref, ref, ag_send.at[which, kind, ch], ag_recv.at[which, kind, ch],
            device_id=target, device_id_type=MESH,
        )

    def arriving(which, kind, ch):
        buf, me = ((PZ, z), (QX, x))[which]
        blk = (me - 1, me + 1, me - 2, me + 2)[kind]
        col = ch * DC + (H if kind == 3 else 0)
        width = DC if kind < 2 else H
        ref = block(buf, blk, col, width)
        return pltpu.make_async_remote_copy(
            ref, ref, ag_send.at[which, kind, ch], ag_recv.at[which, kind, ch],
            device_id=dev(0, 0, 1, 0), device_id_type=MESH,
        )

    def own_sends(ch):
        for which in (0, 1):
            ring(which, 0, ch).start()
            ring(which, 1, ch).start()

    def spread(kind, src, dst, wide):
        def body(n, carry):
            a, yy, cc, r = order(n)

            @pl.when(r > 0)
            def _():
                neg = (lax.rem(4 - a, 4), lax.rem(NY - yy, NY), lax.rem(NC - cc, NC))
                target = dev(neg[0], neg[1], 0, neg[2]) if kind == 0 else dev(0, yy, a, cc)
                pltpu.make_async_remote_copy(
                    src.at[0], dst.at[r], small_send.at[wide], small_recv.at[wide],
                    device_id=target, device_id_type=MESH,
                ).start()

            return carry

        lax.fori_loop(0, R, body, 0)

    def spread_all(dst, wide):
        return pltpu.make_async_remote_copy(
            dst.at[pl.ds(1, R - 1)], dst.at[pl.ds(1, R - 1)], small_send.at[wide], small_recv.at[wide],
            device_id=dev(1, 0, 0, 0), device_id_type=MESH,
        )

    def fold(ref):
        values = ref[...]
        keep = iota(values.shape, 2) // 16 == iota(values.shape, 0)
        return jnp.sum(jnp.where(keep, values, 0.0), axis=0)

    def x_peer(src, dst, send, recv, dx):
        return pltpu.make_async_remote_copy(
            src.at[dx], dst.at[dx], send.at[dx], recv.at[dx], device_id=dev(dx, 0, 0, 0), device_id_type=MESH
        )

    def gather_matrix(index, slot):
        n = iota((S, 1), 0)
        want = to_column(index).astype(jnp.int32) + lax.rem(n, 16) // 4 * ROWS
        gather[slot] = (want == iota((S, 4 * ROWS), 1)).astype(BF16)

    def hard_starts(kind, ch):
        src, dst = ((SP, RP), (SQ, RQ))[kind]

        def body(n, carry):
            a, yy, cc, r = order(n)

            @pl.when(r > 0)
            def _():
                target = dev(a, yy, 0, cc) if kind == 0 else dev(0, yy, a, cc)
                pltpu.make_async_remote_copy(
                    src.at[pl.ds(r * 16, 16), pl.ds(ch * DC, DC)], dst.at[pl.ds(r * 16, 16), pl.ds(ch * DC, DC)],
                    hard_send.at[kind, ch], hard_recv.at[kind, ch], device_id=target, device_id_type=MESH,
                ).start()

            return carry

        lax.fori_loop(0, R, body, 0)

    def hard_all(kind, ch):
        src, dst = ((SP, RP), (SQ, RQ))[kind]
        ref = lambda buf: buf.at[pl.ds(16, S - 16), pl.ds(ch * DC, DC)]
        return pltpu.make_async_remote_copy(
            ref(src), ref(dst), hard_send.at[kind, ch], hard_recv.at[kind, ch],
            device_id=dev(1, 0, 0, 0), device_id_type=MESH,
        )

    def tiles(start, length, body):
        def step(t, carry):
            body(pl.ds(pl.multiple_of(start + t * TN, 128), TN))
            return carry

        lax.fori_loop(0, length // TN, step, 0)

    def serve(kind, ch):
        src, out, mine = ((PZ, SP, RP), (QX, SQ, RQ))[kind]

        def body(cols):
            rows = mm(gather[kind], src[:, cols]).astype(BF16)
            out[:, cols] = rows
            mine[0:16, cols] = rows[0:16]

        tiles(ch * DC, DC, body)

    me_rows = pl.ds(x * ROWS, ROWS)
    par_rows = pl.ds(lax.rem(x + 2, 4) * ROWS, ROWS)
    s_own[...] = jnp.zeros_like(s_own)
    s_par[...] = jnp.zeros_like(s_par)
    hs[...] = jnp.zeros_like(hs)

    def score(acc, rows, keys, ch):
        def body(cols):
            acc[...] += mm_t(QX[rows, cols], keys[:, cols])

        tiles(ch * DC, DC, body)

    def forward(ch):
        for which in (0, 1):
            for kind in (0, 1):
                arriving(which, kind, ch).wait_recv()
                ring(which, kind + 2, ch).start()

    own_sends(0)
    spread(0, w_s, w_r, 0)
    for dx in range(1, 4):
        x_peer(xt_s, xt_r, xt_send, xt_recv, dx).start()
    own_sends(1)
    spread_all(w_r, 0).wait_recv()
    gather_matrix(fold(w_r), 0)
    forward(0)
    own_sends(2)
    for dx in range(1, 4):
        x_peer(xt_s, xt_r, xt_send, xt_recv, dx).wait_recv()
    tables = (xt_r[0] + xt_r[1] + xt_r[2] + xt_r[3])[0:1, :].astype(jnp.int32)
    j_all = (tables // ROWS).astype(F32)
    gather_matrix(lax.rem(tables, ROWS).astype(F32), 1)

    for ch in range(NCH):
        if ch + 1 < NCH:
            forward(ch + 1)
        if ch + 3 < NCH:
            own_sends(ch + 3)
        for kind in (0, 1):
            arriving(kind, 2, ch).wait_recv()
            arriving(kind, 3, ch).wait_recv()
            serve(kind, ch)
            hard_starts(kind, ch)
        score(s_own, me_rows, PZ, ch)
        score(s_par, par_rows, PZ, ch)

    base = (xh * 4 * ROWS).astype(F32)
    lane_p = iota((ROWS, 4 * ROWS), 1).astype(F32)
    pos_own = to_column(pos_row) - base
    pos_par = to_column(xt_r[2][1:2, 0:ROWS]) - base

    def half_stats(acc, pos):
        s = acc[...] * LOGIT_SCALE
        m = jnp.max(s, axis=1, keepdims=True)
        l = jnp.sum(jnp.exp(s - m), axis=1, keepdims=True)
        sp = jnp.sum(jnp.where(lane_p == pos, s, 0.0), axis=1, keepdims=True)
        return m, l, sp

    lane128 = iota((ROWS, 128), 1)
    m_p, l_p, sp_p = half_stats(s_par, pos_par)
    st_s[...] = jnp.where(lane128 == 0, m_p, jnp.where(lane128 == 1, l_p, jnp.where(lane128 == 2, sp_p, 0.0)))

    def pair(src, dst, i):
        return pltpu.make_async_remote_copy(
            src, dst, pair_send.at[i], pair_recv.at[i], device_id=dev(2, 0, 0, 0), device_id_type=MESH
        )

    pair(st_s, st_r, 0).start()
    m_o, l_o, sp_o = half_stats(s_own, pos_own)

    for ch in range(NCH):
        hard_all(0, ch).wait_recv()
        score(hs, me_rows, RP, ch)
    pair(st_s, st_r, 0).wait_recv()
    stats = st_r[...]
    m_r, l_r, sp_r = stats[:, 0:1], stats[:, 1:2], stats[:, 2:3]
    scaled = hs[...] * LOGIT_SCALE + shift
    mask = [codes[k] == codes_p for k in range(3)]
    hard_k = [jnp.sum(jnp.where(mask[k], scaled, 0.0), axis=1, keepdims=True) for k in range(3)]
    present = [jnp.where(owner[k] >= 0, hard_k[k], NEG) for k in range(3)]
    top = jnp.maximum(jnp.maximum(m_o, m_r), jnp.maximum(jnp.maximum(present[0], present[1]), present[2]))
    total = l_o * jnp.exp(m_o - top) + l_r * jnp.exp(m_r - top)
    for k in range(3):
        total = total + jnp.exp(present[k] - top)
    lse = top + jnp.log(total)
    lse_s[...] = jnp.broadcast_to(lse, (ROWS, 128))
    pair(lse_s, lse_r, 1).start()
    loss_ref[...] = to_row(lse - (sp_o + sp_r))
    hard_coef = [jnp.exp(present[k] - lse) for k in range(3)]

    for dx in range(4):
        row = pick(codes_q(dx), hard_coef)
        cx_s[dx] = row
        if dx == 0:
            cx_r[0] = row
    for dx in range(1, 4):
        x_peer(cx_s, cx_r, cx_send, cx_recv, dx).start()

    def half_coef(acc, pos, row_lse, out, column):
        f = jnp.exp(acc[...] * LOGIT_SCALE - row_lse) - jnp.where(lane_p == pos, 1.0, 0.0)
        out[...] = f.astype(BF16)
        coef_t[:, column * ROWS : (column + 1) * ROWS] = jnp.transpose(f).astype(BF16)

    half_coef(s_own, pos_own, lse, coef_o, 0)
    pair(lse_s, lse_r, 1).wait_recv()
    half_coef(s_par, pos_par, lse_r[:, 0:1], coef_p, 1)

    def passage_part(offset, cols):
        ct = coef_t[pl.ds(lax.rem(z + offset, 4) * ROWS, ROWS), :]
        part = mm(ct[:, 0:ROWS], QX[me_rows, cols]) + mm(ct[:, ROWS : 2 * ROWS], QX[par_rows, cols])
        return part * LOGIT_SCALE

    def rs(src, dst, i, step, start, length):
        return pltpu.make_async_remote_copy(
            src.at[:, pl.ds(start, length)], dst.at[:, pl.ds(start, length)], rs_send.at[i], rs_recv.at[i],
            device_id=dev(0, 0, step, 0), device_id_type=MESH,
        )

    far_up = rs(rs_a, rr_a, 0, 1, 0, HD)
    far_dn = rs(rs_a, rr_a, 1, 3, HD, HD)
    up_free = rs(rs_up, rr_up, 2, 1, HD, HD)
    dn_free = rs(rs_dn, rr_dn, 3, 3, 0, HD)
    up_last = rs(rs_up, rr_up, 4, 1, 0, HD)
    dn_last = rs(rs_dn, rr_dn, 5, 3, HD, HD)

    def far(cols):
        rs_a[:, cols] = passage_part(2, cols).astype(BF16)

    tiles(0, HD, far)
    far_up.start()
    tiles(HD, HD, far)
    far_dn.start()

    def partner_part(cols):
        gx_s[:, cols] = (mm(coef_p[...], PZ[:, cols]) * LOGIT_SCALE).astype(BF16)

    tiles(0, D, partner_part)
    pair(gx_s, gx_r, 2).start()

    def up_part(cols):
        rs_up[:, cols] = passage_part(1, cols).astype(BF16)

    def dn_part(cols):
        rs_dn[:, cols] = passage_part(3, cols).astype(BF16)

    tiles(HD, HD, up_part)
    up_free.start()
    tiles(0, HD, dn_part)
    dn_free.start()

    for dx in range(1, 4):
        x_peer(cx_s, cx_r, cx_send, cx_recv, dx).wait_recv()
    c_row = cx_r[0] + cx_r[1] + cx_r[2] + cx_r[3]
    both = jnp.where(iota((2, S), 0) == 0, c_row, j_all)
    c_s[0] = both
    c_r[0] = both
    spread(1, c_s, c_r, 1)

    far_up.wait_recv()

    def up_sum(cols):
        rs_up[:, cols] = (passage_part(1, cols) + rr_a[:, cols].astype(F32)).astype(BF16)

    tiles(0, HD, up_sum)
    up_last.start()
    far_dn.wait_recv()

    def dn_sum(cols):
        rs_dn[:, cols] = (passage_part(3, cols) + rr_a[:, cols].astype(F32)).astype(BF16)

    tiles(HD, HD, dn_sum)
    dn_last.start()

    h = jnp.zeros((ROWS, S), F32)
    for k in range(3):
        h = h + jnp.where(mask[k], hard_coef[k], 0.0)
    hmat[...] = h.astype(BF16)
    pair(gx_s, gx_r, 2).wait_recv()

    def query_grad(cols):
        part = mm(coef_o[...], PZ[:, cols]) + mm(hmat[...], RP[:, cols])
        gq_ref[:, cols] = part * LOGIT_SCALE + gx_r[:, cols].astype(F32)

    tiles(0, D, query_grad)
    gq_out = pltpu.make_async_copy(gq_ref, gq_hbm, out_sem.at[0])
    gq_out.start()

    spread_all(c_r, 1).wait_recv()
    both = fold(c_r)
    hmat[...] = jnp.where(query_number == both[1:2, :], both[0:1, :], 0.0).astype(BF16)
    for ch in range(NCH):
        hard_all(1, ch).wait_recv()

        def passage_grad(cols):
            gp_ref[:, cols] = passage_part(0, cols) + LOGIT_SCALE * mm(hmat[...], RQ[:, cols])

        tiles(ch * DC, DC, passage_grad)
    up_free.wait_recv()
    dn_free.wait_recv()
    up_last.wait_recv()
    dn_last.wait_recv()

    def last(cols):
        gp_ref[:, cols] += rr_up[:, cols].astype(F32) + rr_dn[:, cols].astype(F32)

    outs = [gq_out]
    for ch in range(4):
        tiles(ch * D // 4, D // 4, last)
        cols = pl.ds(ch * D // 4, D // 4)
        outs.append(pltpu.make_async_copy(gp_ref.at[:, cols], gp_hbm.at[:, cols], out_sem.at[1 + ch]))
        outs[-1].start()

    for ch in range(NCH):
        for which in (0, 1):
            for kind in range(4):
                ring(which, kind, ch).wait_send()
            hard_all(which, ch).wait_send()
    for dx in range(1, 4):
        x_peer(xt_s, xt_r, xt_send, xt_recv, dx).wait_send()
        x_peer(cx_s, cx_r, cx_send, cx_recv, dx).wait_send()
    spread_all(w_r, 0).wait_send()
    spread_all(c_r, 1).wait_send()
    pair(st_s, st_r, 0).wait_send()
    pair(lse_s, lse_r, 1).wait_send()
    pair(gx_s, gx_r, 2).wait_send()
    for copy in (far_up, far_dn, up_free, dn_free, up_last, dn_last):
        copy.wait_send()
    for copy in outs:
        copy.wait()


def results(loss_in, gq_in, gp_in, loss_out, gq_out, gp_out):
    loss_out[...] = loss_in[...]
    gq_out[...] = gq_in[...]
    gp_out[...] = gp_in[...]


def on_device(ngrp, queries, passages, positives, hard_owner, hard_row):
    D = queries.shape[1]
    NC = 2 if ngrp % 4 == 0 else 1
    NY = ngrp // (2 * NC)
    R = 4 * NY * NC
    S = 16 * R
    shift = math.log(8 * ROWS / 3)
    vmem = pltpu.VMEM
    dma = pltpu.SemaphoreType.DMA
    wide = vmem((ROWS, D), BF16)
    any_spec = pl.BlockSpec(memory_space=pl.ANY)
    vmem_spec = pl.BlockSpec(memory_space=pltpu.VMEM)
    loss, gq, gp = pl.pallas_call(
        functools.partial(kernel, NY, NC, D, shift),
        out_shape=(
            jax.ShapeDtypeStruct((1, ROWS), F32),
            jax.ShapeDtypeStruct((ROWS, D), F32),
            jax.ShapeDtypeStruct((ROWS, D), F32),
        ),
        in_specs=[any_spec, any_spec, vmem_spec, vmem_spec, vmem_spec],
        out_specs=(vmem_spec, any_spec, any_spec),
        scratch_shapes=[
            vmem((4 * ROWS, D), BF16), vmem((4 * ROWS, D), BF16),
            vmem((S, D), BF16), vmem((S, D), BF16), vmem((S, D), BF16), vmem((S, D), BF16),
            wide, wide, wide, wide, wide, wide, wide, wide,
            vmem((ROWS, 4 * ROWS), F32), vmem((ROWS, 4 * ROWS), F32), vmem((ROWS, S), F32),
            vmem((2, S, 4 * ROWS), BF16),
            vmem((ROWS, 4 * ROWS), BF16), vmem((ROWS, 4 * ROWS), BF16), vmem((4 * ROWS, 2 * ROWS), BF16),
            vmem((ROWS, S), BF16),
            vmem((4, 2, S), F32), vmem((4, 2, S), F32),
            vmem((1, 1, S), F32), vmem((R, 1, S), F32),
            vmem((4, 1, S), F32), vmem((4, 1, S), F32),
            vmem((1, 2, S), F32), vmem((R, 2, S), F32),
            vmem((ROWS, 128), F32), vmem((ROWS, 128), F32), vmem((ROWS, 128), F32), vmem((ROWS, 128), F32),
            vmem((ROWS, D), F32), vmem((ROWS, D), F32),
            dma((2,)), dma((5,)), dma((2, 4, NCH)), dma((2, 4, NCH)), dma((2, NCH)), dma((2, NCH)),
            dma((4,)), dma((4,)), dma((4,)), dma((4,)), dma((2,)), dma((2,)), dma((3,)), dma((3,)),
            dma((6,)), dma((6,)),
        ],
        compiler_params=pltpu.CompilerParams(
            collective_id=0, has_side_effects=True, vmem_limit_bytes=60 * 2**20
        ),
        cost_estimate=pl.CostEstimate(flops=9 * 10**9, bytes_accessed=8 * 2**20, transcendentals=2 * 10**5),
        name="infonce",
    )(queries, passages, positives, hard_owner.T, hard_row.T)
    block = pl.BlockSpec((ROWS // 4, D), lambda i: (i, 0))
    row = pl.BlockSpec((1, ROWS), lambda i: (0, 0))
    loss, gq, gp = pl.pallas_call(
        results,
        grid=(4,),
        in_specs=[row, block, block],
        out_specs=(row, block, block),
        out_shape=tuple(jax.ShapeDtypeStruct(a.shape, F32) for a in (loss, gq, gp)),
        name="results",
    )(loss, gq, gp)
    return loss.reshape(ROWS), gq, gp


def solution(mesh):
    return jax.shard_map(
        functools.partial(on_device, mesh.shape["grp"]),
        mesh=mesh,
        in_specs=(
            P(("grp", "blk"), None),
            P(("grp", "blk"), None),
            P("grp", "blk"),
            P(("grp", "blk"), None),
            P(("grp", "blk"), None),
        ),
        out_specs=(P(("grp", "blk")), P(("grp", "blk"), None), P(("grp", "blk"), None)),
        check_vma=False,
    )
```

```python
import functools
import math

import jax
import jax.numpy as jnp
from jax import lax
from jax.experimental import pallas as pl
from jax.experimental.pallas import tpu as pltpu
from jax.sharding import PartitionSpec as P

LOGIT_SCALE = 20.0
ROWS = 128
CAP = 4
NCH = 4
EARLY = (1, 2)
NEG = -1e30
MESH = pl.DeviceIdType.MESH
F32 = jnp.float32
BF16 = jnp.bfloat16


def iota(shape, dim):
    return lax.broadcasted_iota(jnp.int32, shape, dim)


def to_column(row):
    n = row.shape[1]
    eye = iota((n, n), 0) == iota((n, n), 1)
    return jnp.sum(jnp.where(eye, row, jnp.zeros_like(row)), axis=1, keepdims=True)


def to_row(col):
    n = col.shape[0]
    eye = iota((n, n), 0) == iota((n, n), 1)
    return jnp.sum(jnp.where(eye, col, jnp.zeros_like(col)), axis=0, keepdims=True)


def mm(a, b):
    return jnp.dot(a, b, preferred_element_type=F32)


def mm_t(a, b):
    return lax.dot_general(a, b, (((1,), (1,)), ((), ())), preferred_element_type=F32)


def kernel(
    NY, NC, D, shift,
    q_hbm, p_hbm, pos_ref, own_ref, row_ref,
    loss_ref, gq_hbm, gp_hbm,
    PZ, QX, SP, SQ, RP, MQ, RQ,
    rs_a, rs_up, rs_dn, rr_a, rr_up, rr_dn, gx_s, gx_r,
    s_own, s_par, hs, gather, coef_o, coef_p, coef_t, hmat,
    xt_s, xt_r, w_s, w_r, cx_s, cx_r, cz_s, cz_r, c_s, c_r, st_s, st_r, lse_s, lse_r, gq_ref, gp_ref,
    in_sem, out_sem, ag_send, ag_recv, hard_send, hard_recv,
    xt_send, xt_recv, cx_send, cx_recv, cz_send, cz_recv, turn_send, turn_recv, small_send, small_recv, pair_send, pair_recv, rs_send, rs_recv,
):
    R = 4 * NY * NC
    S = 16 * R
    HR = S // 4
    SECOND = [0] + sorted(range(1, NY * NC), key=lambda m: (m % NC, m // NC == 2, m))
    DC = D // NCH
    H = DC // 2
    HD = D // 2
    TN = min(512, H)
    g = lax.axis_index("grp")
    b = lax.axis_index("blk")
    z = lax.rem(b, 4)
    xh = b // 4
    c = lax.rem(g, NC)
    x = xh * 2 + lax.rem(g // NC, 2)
    y = g // (2 * NC)

    def dev(dx, dy, dz, dc):
        x2 = lax.rem(x + dx, 4)
        y2 = lax.rem(y + dy, NY)
        z2 = lax.rem(z + dz, 4)
        c2 = lax.rem(c + dc, NC)
        return ((y2 * 2 + lax.rem(x2, 2)) * NC + c2, (x2 // 2) * 4 + z2)

    def order(n):
        cc = lax.rem(n, NC)
        i = lax.rem(n // NC, 4)
        s = n // (4 * NC)
        a = lax.rem(1 + 2 * i + i // 2, 4)
        yy = lax.rem(a + s + 1, NY)
        return a, yy, cc, (a * NY + yy) * NC + cc

    p_in = pltpu.make_async_copy(p_hbm, PZ.at[pl.ds(z * ROWS, ROWS)], in_sem.at[0])
    q_in = pltpu.make_async_copy(q_hbm, QX.at[pl.ds(x * ROWS, ROWS)], in_sem.at[1])
    p_in.start()
    q_in.start()
    barrier = pltpu.get_barrier_semaphore()

    def greet(n, carry):
        a, yy, cc, r = order(n)

        @pl.when(r > 0)
        def _():
            pl.semaphore_signal(barrier, inc=1, device_id=dev(a, yy, 0, cc), device_id_type=MESH)

        return carry

    lax.fori_loop(0, R, greet, 0)
    for dz in range(1, 4):
        pl.semaphore_signal(barrier, inc=1, device_id=dev(0, 0, dz, 0), device_id_type=MESH)
    lane = iota((1, S), 1)
    slot_r = lane // 16
    slot_b = lax.rem(lane, 16) // 4
    slot_t = lax.rem(lane, 4)
    r_a = slot_r // (NY * NC)
    r_y = lax.rem(slot_r // NC, NY)
    r_c = lax.rem(slot_r, NC)

    def dev_id(x2, y2, z2, c2):
        return ((y2 * 2 + lax.rem(x2, 2)) * NC + c2) * 8 + (x2 // 2) * 4 + z2

    owner = [to_column(own_ref[k : k + 1, :].astype(F32)) for k in range(3)]
    hrow = [to_column(row_ref[k : k + 1, :].astype(F32)) for k in range(3)]
    ndev = 8 * 2 * NY * NC
    lane_o = iota((ROWS, max(ndev, 128)), 1).astype(F32)
    hot = [(owner[k] == lane_o).astype(F32) for k in range(3)]
    count = hot[0] + hot[1] + hot[2]
    lower = (iota((ROWS, ROWS), 1) < iota((ROWS, ROWS), 0)).astype(BF16)
    before = mm(lower, count.astype(BF16))
    rank = [jnp.sum(h * before, axis=1, keepdims=True) for h in hot]
    codes = [jnp.where(owner[k] >= 0, owner[k] * CAP + rank[k], -1.0) for k in range(3)]
    codes_p = (
        dev_id(lax.rem(x + 4 - r_a, 4), lax.rem(y + NY - r_y, NY), slot_b, lax.rem(c + NC - r_c, NC)) * CAP + slot_t
    ).astype(F32)

    def codes_q(dx):
        full = dev_id(lax.rem(x + dx, 4), lax.rem(y + r_y, NY), lax.rem(z + r_a, 4), lax.rem(c + r_c, NC)) * CAP + slot_t
        return jnp.where(slot_b == x, full, -2).astype(F32)

    def pick(code_row, values):
        total = jnp.zeros((ROWS, S), F32)
        for k in range(3):
            total = total + jnp.where(codes[k] == code_row, values[k], 0.0)
        return jnp.sum(total, axis=0, keepdims=True)

    w_row = pick(codes_p, hrow)
    w_s[0] = w_row
    w_r[0] = w_row
    query_number = iota((ROWS, 1), 0).astype(F32)
    query_and_row = [query_number + ROWS * hrow[k] for k in range(3)]
    pos_row = pos_ref[...].astype(F32)
    pos_wide = jnp.concatenate([pos_row] + [jnp.zeros((1, S - ROWS), F32)], axis=1)
    for dx in range(4):
        table = jnp.where(iota((2, S), 0) == 0, pick(codes_q(dx), query_and_row), pos_wide)
        xt_s[dx] = table
        if dx == 0:
            xt_r[0] = table

    pl.semaphore_wait(barrier, R - 1 + 3)
    p_in.wait()
    q_in.wait()

    def block(buf, i, col, width):
        return buf.at[pl.ds(lax.rem(i + 4, 4) * ROWS, ROWS), pl.ds(col, width)]

    def ring(which, kind, ch):
        buf, me = ((PZ, z), (QX, x))[which]
        step = 1 if kind in (0, 2) else 3
        blk = me if kind < 2 else (me - 1 if kind == 2 else me + 1)
        col = ch * DC + (H if kind == 3 else 0)
        width = DC if kind < 2 else H
        ref = block(buf, blk, col, width)
        target = dev(0, 0, step, 0) if which == 0 else dev(step, 0, 0, 0)
        return pltpu.make_async_remote_copy(
            ref, ref, ag_send.at[which, kind, ch], ag_recv.at[which, kind, ch],
            device_id=target, device_id_type=MESH,
        )

    def arriving(which, kind, ch):
        buf, me = ((PZ, z), (QX, x))[which]
        blk = (me - 1, me + 1, me - 2, me + 2)[kind]
        col = ch * DC + (H if kind == 3 else 0)
        width = DC if kind < 2 else H
        ref = block(buf, blk, col, width)
        return pltpu.make_async_remote_copy(
            ref, ref, ag_send.at[which, kind, ch], ag_recv.at[which, kind, ch],
            device_id=dev(0, 0, 1, 0), device_id_type=MESH,
        )

    def own_sends(ch):
        for which in (0, 1):
            ring(which, 0, ch).start()
            ring(which, 1, ch).start()

    def ask(n, carry):
        a, yy, cc, r = order(n)

        @pl.when(r > 0)
        def _():
            target = dev(lax.rem(4 - a, 4), lax.rem(NY - yy, NY), 0, lax.rem(NC - cc, NC))
            pltpu.make_async_remote_copy(
                w_s.at[0], w_r.at[r], small_send.at[0], small_recv.at[0], device_id=target, device_id_type=MESH
            ).start()

        return carry

    def asked():
        ref = w_r.at[pl.ds(1, R - 1)]
        return pltpu.make_async_remote_copy(
            ref, ref, small_send.at[0], small_recv.at[0], device_id=dev(1, 0, 0, 0), device_id_type=MESH
        )

    def z_peer(dz):
        return pltpu.make_async_remote_copy(
            cz_s.at[0], cz_r.at[dz], cz_send.at[dz], cz_recv.at[dz], device_id=dev(0, 0, dz, 0), device_id_type=MESH
        )

    def yc_peer(m):
        return pltpu.make_async_remote_copy(
            c_s.at[0], c_r.at[m], small_send.at[1], small_recv.at[1],
            device_id=dev(0, m // NC, 0, m % NC), device_id_type=MESH,
        )

    def yc_all():
        ref = c_r.at[pl.ds(1, NY * NC - 1)]
        return pltpu.make_async_remote_copy(
            ref, ref, small_send.at[1], small_recv.at[1], device_id=dev(1, 0, 0, 0), device_id_type=MESH
        )

    def fold(ref, group):
        values = ref[...]
        total = jnp.zeros(values.shape[1:], F32)
        for n in range(values.shape[0]):
            total = total + jnp.where(group == n, values[n], 0.0)
        return total

    slot_number = slot_r

    def x_peer(src, dst, send, recv, dx):
        return pltpu.make_async_remote_copy(
            src.at[dx], dst.at[dx], send.at[dx], recv.at[dx], device_id=dev(dx, 0, 0, 0), device_id_type=MESH
        )

    def gather_matrix(index, slot):
        n = iota((S, 1), 0)
        want = to_column(index).astype(jnp.int32) + lax.rem(n, 16) // 4 * ROWS
        gather[slot] = (want == iota((S, 4 * ROWS), 1)).astype(BF16)

    def hard_starts(ch):
        def body(n, carry):
            a, yy, cc, r = order(n)

            @pl.when(r > 0)
            def _():
                pltpu.make_async_remote_copy(
                    SP.at[pl.ds(r * 16, 16), pl.ds(ch * DC, DC)], RP.at[pl.ds(r * 16, 16), pl.ds(ch * DC, DC)],
                    hard_send.at[0, ch], hard_recv.at[0, ch], device_id=dev(a, yy, 0, cc), device_id_type=MESH,
                ).start()

            return carry

        lax.fori_loop(0, R, body, 0)

    def hard_all(kind, ch):
        cols = pl.ds(ch * DC, DC)
        ref = RP.at[pl.ds(16, S - 16), cols] if kind == 0 else RQ.at[:, pl.ds(16, HR - 16), cols]
        return pltpu.make_async_remote_copy(
            ref, ref, hard_send.at[kind, ch], hard_recv.at[kind, ch], device_id=dev(1, 0, 0, 0), device_id_type=MESH
        )

    def turn(dz, ch):
        cols = pl.ds(ch * DC, DC)
        return pltpu.make_async_remote_copy(
            SQ.at[dz, :, cols], MQ.at[dz, :, cols], turn_send.at[dz, ch], turn_recv.at[dz, ch],
            device_id=dev(0, 0, dz, 0), device_id_type=MESH,
        )

    def second(ch):
        cols = pl.ds(ch * DC, DC)
        for dz in range(1, 4):
            turn(dz, ch).wait_recv()
        for m in SECOND[1:]:
            part = pl.ds(m * 16, 16)
            pltpu.make_async_remote_copy(
                MQ.at[:, part, cols], RQ.at[:, part, cols], hard_send.at[1, ch], hard_recv.at[1, ch],
                device_id=dev(0, m // NC, 0, m % NC), device_id_type=MESH,
            ).start()
        RQ[:, 0:16, cols] = MQ[:, 0:16, cols]

    def tiles(start, length, body):
        def step(t, carry):
            body(pl.ds(pl.multiple_of(start + t * TN, 128), TN))
            return carry

        lax.fori_loop(0, length // TN, step, 0)

    def serve_p(cols):
        rows = mm(gather[0], PZ[:, cols]).astype(BF16)
        SP[:, cols] = rows
        RP[0:16, cols] = rows[0:16]

    def serve_q(cols):
        rows = mm(gather[1], QX[:, cols]).astype(BF16)
        for dz in range(4):
            (MQ if dz == 0 else SQ)[dz, :, cols] = rows[dz * HR : (dz + 1) * HR]

    me_rows = pl.ds(x * ROWS, ROWS)
    par_rows = pl.ds(lax.rem(x + 2, 4) * ROWS, ROWS)
    s_own[...] = jnp.zeros_like(s_own)
    s_par[...] = jnp.zeros_like(s_par)
    hs[...] = jnp.zeros_like(hs)

    def score(acc, rows, keys, ch):
        def body(cols):
            acc[...] += mm_t(QX[rows, cols], keys[:, cols])

        tiles(ch * DC, DC, body)

    def forward(ch):
        for which in (0, 1):
            for kind in (0, 1):
                arriving(which, kind, ch).wait_recv()
                ring(which, kind + 2, ch).start()

    own_sends(0)
    lax.fori_loop(0, R, ask, 0)
    for dx in range(1, 4):
        x_peer(xt_s, xt_r, xt_send, xt_recv, dx).start()
    own_sends(1)
    asked().wait_recv()
    gather_matrix(fold(w_r, slot_number), 0)
    forward(0)
    own_sends(2)
    for dx in range(1, 4):
        x_peer(xt_s, xt_r, xt_send, xt_recv, dx).wait_recv()
    tables = (xt_r[0] + xt_r[1] + xt_r[2] + xt_r[3])[0:1, :].astype(jnp.int32)
    j_all = (tables // ROWS).astype(F32)
    gather_matrix(lax.rem(tables, ROWS).astype(F32), 1)

    for ch in range(NCH):
        if ch + 1 < NCH:
            forward(ch + 1)
        if ch + 3 < NCH:
            own_sends(ch + 3)
        arriving(0, 2, ch).wait_recv()
        arriving(0, 3, ch).wait_recv()
        tiles(ch * DC, DC, serve_p)
        hard_starts(ch)
        arriving(1, 2, ch).wait_recv()
        arriving(1, 3, ch).wait_recv()
        tiles(ch * DC, DC, serve_q)
        for dz in (1, 3, 2):
            turn(dz, ch).start()
        score(s_own, me_rows, PZ, ch)
        score(s_par, par_rows, PZ, ch)

    base = (xh * 4 * ROWS).astype(F32)
    lane_p = iota((ROWS, 4 * ROWS), 1).astype(F32)
    pos_own = to_column(pos_row) - base
    pos_par = to_column(xt_r[2][1:2, 0:ROWS]) - base

    def half_stats(acc, pos):
        s = acc[...] * LOGIT_SCALE
        m = jnp.max(s, axis=1, keepdims=True)
        l = jnp.sum(jnp.exp(s - m), axis=1, keepdims=True)
        sp = jnp.sum(jnp.where(lane_p == pos, s, 0.0), axis=1, keepdims=True)
        return m, l, sp

    lane128 = iota((ROWS, 128), 1)
    m_p, l_p, sp_p = half_stats(s_par, pos_par)
    st_s[...] = jnp.where(lane128 == 0, m_p, jnp.where(lane128 == 1, l_p, jnp.where(lane128 == 2, sp_p, 0.0)))

    def pair(src, dst, i):
        return pltpu.make_async_remote_copy(
            src, dst, pair_send.at[i], pair_recv.at[i], device_id=dev(2, 0, 0, 0), device_id_type=MESH
        )

    pair(st_s, st_r, 0).start()
    m_o, l_o, sp_o = half_stats(s_own, pos_own)

    for ch in range(NCH):
        hard_all(0, ch).wait_recv()
        score(hs, me_rows, RP, ch)
        if ch in EARLY:
            second(EARLY.index(ch))
    pair(st_s, st_r, 0).wait_recv()
    stats = st_r[...]
    m_r, l_r, sp_r = stats[:, 0:1], stats[:, 1:2], stats[:, 2:3]
    scaled = hs[...] * LOGIT_SCALE + shift
    mask = [codes[k] == codes_p for k in range(3)]
    hard_k = [jnp.sum(jnp.where(mask[k], scaled, 0.0), axis=1, keepdims=True) for k in range(3)]
    present = [jnp.where(owner[k] >= 0, hard_k[k], NEG) for k in range(3)]
    top = jnp.maximum(jnp.maximum(m_o, m_r), jnp.maximum(jnp.maximum(present[0], present[1]), present[2]))
    total = l_o * jnp.exp(m_o - top) + l_r * jnp.exp(m_r - top)
    for k in range(3):
        total = total + jnp.exp(present[k] - top)
    lse = top + jnp.log(total)
    lse_s[...] = jnp.broadcast_to(lse, (ROWS, 128))
    pair(lse_s, lse_r, 1).start()
    loss_ref[...] = to_row(lse - (sp_o + sp_r))
    hard_coef = [jnp.exp(present[k] - lse) for k in range(3)]

    def half_coef(acc, pos, row_lse, out, column):
        f = jnp.exp(acc[...] * LOGIT_SCALE - row_lse) - jnp.where(lane_p == pos, 1.0, 0.0)
        out[...] = f.astype(BF16)
        coef_t[:, column * ROWS : (column + 1) * ROWS] = jnp.transpose(f).astype(BF16)

    half_coef(s_own, pos_own, lse, coef_o, 0)
    pair(lse_s, lse_r, 1).wait_recv()
    half_coef(s_par, pos_par, lse_r[:, 0:1], coef_p, 1)

    def passage_part(offset, cols):
        ct = coef_t[pl.ds(lax.rem(z + offset, 4) * ROWS, ROWS), :]
        part = mm(ct[:, 0:ROWS], QX[me_rows, cols]) + mm(ct[:, ROWS : 2 * ROWS], QX[par_rows, cols])
        return part * LOGIT_SCALE

    def rs(src, dst, i, step, start, length):
        return pltpu.make_async_remote_copy(
            src.at[:, pl.ds(start, length)], dst.at[:, pl.ds(start, length)], rs_send.at[i], rs_recv.at[i],
            device_id=dev(0, 0, step, 0), device_id_type=MESH,
        )

    far_up = rs(rs_a, rr_a, 0, 1, 0, HD)
    far_dn = rs(rs_a, rr_a, 1, 3, HD, HD)
    up_free = rs(rs_up, rr_up, 2, 1, HD, HD)
    dn_free = rs(rs_dn, rr_dn, 3, 3, 0, HD)
    up_last = rs(rs_up, rr_up, 4, 1, 0, HD)
    dn_last = rs(rs_dn, rr_dn, 5, 3, HD, HD)

    def far(cols):
        rs_a[:, cols] = passage_part(2, cols).astype(BF16)

    tiles(0, HD, far)
    far_up.start()
    tiles(HD, HD, far)
    far_dn.start()

    for dx in range(4):
        row = pick(codes_q(dx), hard_coef)
        cx_s[dx] = row
        if dx == 0:
            cx_r[0] = row
    for dx in range(1, 4):
        x_peer(cx_s, cx_r, cx_send, cx_recv, dx).start()

    def partner_part(cols):
        gx_s[:, cols] = (mm(coef_p[...], PZ[:, cols]) * LOGIT_SCALE).astype(BF16)

    tiles(0, D, partner_part)
    pair(gx_s, gx_r, 2).start()

    def up_part(cols):
        rs_up[:, cols] = passage_part(1, cols).astype(BF16)

    def dn_part(cols):
        rs_dn[:, cols] = passage_part(3, cols).astype(BF16)

    tiles(HD, HD, up_part)
    up_free.start()
    tiles(0, HD, dn_part)
    dn_free.start()

    for dx in range(1, 4):
        x_peer(cx_s, cx_r, cx_send, cx_recv, dx).wait_recv()
    both = jnp.where(iota((2, S), 0) == 0, cx_r[0] + cx_r[1] + cx_r[2] + cx_r[3], j_all)
    cz_s[0] = both
    cz_r[0] = both
    for dz in (1, 3, 2):
        z_peer(dz).start()
    for ch in range(len(EARLY), NCH):
        second(ch)

    far_up.wait_recv()

    def up_sum(cols):
        rs_up[:, cols] = (passage_part(1, cols) + rr_a[:, cols].astype(F32)).astype(BF16)

    tiles(0, HD, up_sum)
    up_last.start()
    far_dn.wait_recv()

    def dn_sum(cols):
        rs_dn[:, cols] = (passage_part(3, cols) + rr_a[:, cols].astype(F32)).astype(BF16)

    tiles(HD, HD, dn_sum)
    dn_last.start()

    for dz in range(1, 4):
        z_peer(dz).wait_recv()
    both = fold(cz_r, r_a)
    c_s[0] = both
    c_r[0] = both
    for m in range(1, NY * NC):
        yc_peer(m).start()

    h = jnp.zeros((ROWS, S), F32)
    for k in range(3):
        h = h + jnp.where(mask[k], hard_coef[k], 0.0)
    hmat[...] = h.astype(BF16)
    pair(gx_s, gx_r, 2).wait_recv()

    def query_grad(cols):
        part = mm(coef_o[...], PZ[:, cols]) + mm(hmat[...], RP[:, cols])
        gq_ref[:, cols] = part * LOGIT_SCALE + gx_r[:, cols].astype(F32)

    tiles(0, D, query_grad)
    gq_out = pltpu.make_async_copy(gq_ref, gq_hbm, out_sem.at[0])
    gq_out.start()

    yc_all().wait_recv()
    both = fold(c_r, r_y * NC + r_c)
    hmat[...] = jnp.where(query_number == both[1:2, :], both[0:1, :], 0.0).astype(BF16)
    for ch in range(NCH):
        hard_all(1, ch).wait_recv()

        def passage_grad(cols):
            gp_ref[:, cols] = passage_part(0, cols) + LOGIT_SCALE * mm(hmat[...], RQ[:, :, cols].reshape(S, TN))

        tiles(ch * DC, DC, passage_grad)
    up_free.wait_recv()
    dn_free.wait_recv()
    up_last.wait_recv()
    dn_last.wait_recv()

    def last(cols):
        gp_ref[:, cols] += rr_up[:, cols].astype(F32) + rr_dn[:, cols].astype(F32)

    outs = [gq_out]
    for ch in range(4):
        tiles(ch * D // 4, D // 4, last)
        cols = pl.ds(ch * D // 4, D // 4)
        outs.append(pltpu.make_async_copy(gp_ref.at[:, cols], gp_hbm.at[:, cols], out_sem.at[1 + ch]))
        outs[-1].start()

    for ch in range(NCH):
        for which in (0, 1):
            for kind in range(4):
                ring(which, kind, ch).wait_send()
            hard_all(which, ch).wait_send()
        for dz in range(1, 4):
            turn(dz, ch).wait_send()
    for dx in range(1, 4):
        x_peer(xt_s, xt_r, xt_send, xt_recv, dx).wait_send()
        x_peer(cx_s, cx_r, cx_send, cx_recv, dx).wait_send()
    for dz in range(1, 4):
        z_peer(dz).wait_send()
    asked().wait_send()
    yc_all().wait_send()
    pair(st_s, st_r, 0).wait_send()
    pair(lse_s, lse_r, 1).wait_send()
    pair(gx_s, gx_r, 2).wait_send()
    for copy in (far_up, far_dn, up_free, dn_free, up_last, dn_last):
        copy.wait_send()
    for copy in outs:
        copy.wait()


def results(loss_in, gq_in, gp_in, loss_out, gq_out, gp_out):
    loss_out[...] = loss_in[...]
    gq_out[...] = gq_in[...]
    gp_out[...] = gp_in[...]


def on_device(ngrp, queries, passages, positives, hard_owner, hard_row):
    D = queries.shape[1]
    NC = 2 if ngrp % 4 == 0 else 1
    NY = ngrp // (2 * NC)
    R = 4 * NY * NC
    S = 16 * R
    shift = math.log(8 * ROWS / 3)
    vmem = pltpu.VMEM
    dma = pltpu.SemaphoreType.DMA
    wide = vmem((ROWS, D), BF16)
    any_spec = pl.BlockSpec(memory_space=pl.ANY)
    vmem_spec = pl.BlockSpec(memory_space=pltpu.VMEM)
    loss, gq, gp = pl.pallas_call(
        functools.partial(kernel, NY, NC, D, shift),
        out_shape=(
            jax.ShapeDtypeStruct((1, ROWS), F32),
            jax.ShapeDtypeStruct((ROWS, D), F32),
            jax.ShapeDtypeStruct((ROWS, D), F32),
        ),
        in_specs=[any_spec, any_spec, vmem_spec, vmem_spec, vmem_spec],
        out_specs=(vmem_spec, any_spec, any_spec),
        scratch_shapes=[
            vmem((4 * ROWS, D), BF16), vmem((4 * ROWS, D), BF16),
            vmem((S, D), BF16), vmem((4, S // 4, D), BF16), vmem((S, D), BF16), vmem((4, S // 4, D), BF16),
            vmem((4, S // 4, D), BF16),
            wide, wide, wide, wide, wide, wide, wide, wide,
            vmem((ROWS, 4 * ROWS), F32), vmem((ROWS, 4 * ROWS), F32), vmem((ROWS, S), F32),
            vmem((2, S, 4 * ROWS), BF16),
            vmem((ROWS, 4 * ROWS), BF16), vmem((ROWS, 4 * ROWS), BF16), vmem((4 * ROWS, 2 * ROWS), BF16),
            vmem((ROWS, S), BF16),
            vmem((4, 2, S), F32), vmem((4, 2, S), F32),
            vmem((1, 1, S), F32), vmem((R, 1, S), F32),
            vmem((4, 1, S), F32), vmem((4, 1, S), F32),
            vmem((1, 2, S), F32), vmem((4, 2, S), F32),
            vmem((1, 2, S), F32), vmem((NY * NC, 2, S), F32),
            vmem((ROWS, 128), F32), vmem((ROWS, 128), F32), vmem((ROWS, 128), F32), vmem((ROWS, 128), F32),
            vmem((ROWS, D), F32), vmem((ROWS, D), F32),
            dma((2,)), dma((5,)), dma((2, 4, NCH)), dma((2, 4, NCH)), dma((2, NCH)), dma((2, NCH)),
            dma((4,)), dma((4,)), dma((4,)), dma((4,)), dma((4,)), dma((4,)), dma((4, NCH)), dma((4, NCH)), dma((2,)), dma((2,)), dma((3,)), dma((3,)),
            dma((6,)), dma((6,)),
        ],
        compiler_params=pltpu.CompilerParams(
            collective_id=0, has_side_effects=True, vmem_limit_bytes=60 * 2**20
        ),
        cost_estimate=pl.CostEstimate(flops=9 * 10**9, bytes_accessed=8 * 2**20, transcendentals=2 * 10**5),
        name="infonce",
    )(queries, passages, positives, hard_owner.T, hard_row.T)
    block = pl.BlockSpec((ROWS // 4, D), lambda i: (i, 0))
    row = pl.BlockSpec((1, ROWS), lambda i: (0, 0))
    loss, gq, gp = pl.pallas_call(
        results,
        grid=(4,),
        in_specs=[row, block, block],
        out_specs=(row, block, block),
        out_shape=tuple(jax.ShapeDtypeStruct(a.shape, F32) for a in (loss, gq, gp)),
        name="results",
    )(loss, gq, gp)
    return loss.reshape(ROWS), gq, gp


def solution(mesh):
    return jax.shard_map(
        functools.partial(on_device, mesh.shape["grp"]),
        mesh=mesh,
        in_specs=(
            P(("grp", "blk"), None),
            P(("grp", "blk"), None),
            P("grp", "blk"),
            P(("grp", "blk"), None),
            P(("grp", "blk"), None),
        ),
        out_specs=(P(("grp", "blk")), P(("grp", "blk"), None), P(("grp", "blk"), None)),
        check_vma=False,
    )
```

```python
import functools
import math

import jax
import jax.numpy as jnp
from jax import lax
from jax.experimental import pallas as pl
from jax.experimental.pallas import tpu as pltpu
from jax.sharding import PartitionSpec as P

LOGIT_SCALE = 20.0
ROWS = 128
CAP = 4
NCH = 4
EARLY = (1, 2)
NEG = -1e30
MESH = pl.DeviceIdType.MESH
F32 = jnp.float32
BF16 = jnp.bfloat16


def iota(shape, dim):
    return lax.broadcasted_iota(jnp.int32, shape, dim)


def to_column(row):
    n = row.shape[1]
    eye = iota((n, n), 0) == iota((n, n), 1)
    return jnp.sum(jnp.where(eye, row, jnp.zeros_like(row)), axis=1, keepdims=True)


def to_row(col):
    n = col.shape[0]
    eye = iota((n, n), 0) == iota((n, n), 1)
    return jnp.sum(jnp.where(eye, col, jnp.zeros_like(col)), axis=0, keepdims=True)


def mm(a, b):
    return jnp.dot(a, b, preferred_element_type=F32)


def mm_t(a, b):
    return lax.dot_general(a, b, (((1,), (1,)), ((), ())), preferred_element_type=F32)


def kernel(
    NY, NC, D, shift,
    q_hbm, p_hbm, pos_ref, own_ref, row_ref,
    loss_ref, gq_hbm, gp_hbm,
    PZ, QX, SP, SQ, MP, RP, MQ, RQ,
    rs_a, rs_up, rs_dn, rr_a, rr_up, rr_dn, gx_s, gx_r,
    s_own, s_par, hs, gather, coef_o, coef_p, coef_t, hmat,
    xt_s, xt_r, w_s, w_r, cx_s, cx_r, cz_s, cz_r, c_s, c_r, st_s, st_r, lse_s, lse_r, gq_ref, gp_ref,
    in_sem, out_sem, ag_send, ag_recv, hard_send, hard_recv,
    xt_send, xt_recv, cx_send, cx_recv, cz_send, cz_recv, turn_send, turn_recv, yc_send, yc_recv, pair_send, pair_recv, rs_send, rs_recv,
):
    R = 4 * NY * NC
    S = 16 * R
    YC = NY * NC
    HR = S // 4
    SECOND = [0] + sorted(range(1, NY * NC), key=lambda m: (m % NC, m // NC == 2, m))
    DC = D // NCH
    H = DC // 2
    HD = D // 2
    TN = min(512, H)
    g = lax.axis_index("grp")
    b = lax.axis_index("blk")
    z = lax.rem(b, 4)
    xh = b // 4
    c = lax.rem(g, NC)
    x = xh * 2 + lax.rem(g // NC, 2)
    y = g // (2 * NC)

    def dev(dx, dy, dz, dc):
        x2 = lax.rem(x + dx, 4)
        y2 = lax.rem(y + dy, NY)
        z2 = lax.rem(z + dz, 4)
        c2 = lax.rem(c + dc, NC)
        return ((y2 * 2 + lax.rem(x2, 2)) * NC + c2, (x2 // 2) * 4 + z2)

    p_in = pltpu.make_async_copy(p_hbm, PZ.at[pl.ds(z * ROWS, ROWS)], in_sem.at[0])
    q_in = pltpu.make_async_copy(q_hbm, QX.at[pl.ds(x * ROWS, ROWS)], in_sem.at[1])
    p_in.start()
    q_in.start()
    barrier = pltpu.get_barrier_semaphore()

    for n in range(1, 4):
        pl.semaphore_signal(barrier, inc=1, device_id=dev(n, 0, 0, 0), device_id_type=MESH)
        pl.semaphore_signal(barrier, inc=1, device_id=dev(0, 0, n, 0), device_id_type=MESH)
    for m in range(1, YC):
        pl.semaphore_signal(barrier, inc=1, device_id=dev(0, m // NC, 0, m % NC), device_id_type=MESH)
    lane = iota((1, S), 1)
    slot_r = lane // 16
    slot_b = lax.rem(lane, 16) // 4
    slot_t = lax.rem(lane, 4)
    r_a = slot_r // (NY * NC)
    r_y = lax.rem(slot_r // NC, NY)
    r_c = lax.rem(slot_r, NC)

    def dev_id(x2, y2, z2, c2):
        return ((y2 * 2 + lax.rem(x2, 2)) * NC + c2) * 8 + (x2 // 2) * 4 + z2

    owner = [to_column(own_ref[k : k + 1, :].astype(F32)) for k in range(3)]
    hrow = [to_column(row_ref[k : k + 1, :].astype(F32)) for k in range(3)]
    ndev = 8 * 2 * NY * NC
    lane_o = iota((ROWS, max(ndev, 128)), 1).astype(F32)
    hot = [(owner[k] == lane_o).astype(F32) for k in range(3)]
    count = hot[0] + hot[1] + hot[2]
    lower = (iota((ROWS, ROWS), 1) < iota((ROWS, ROWS), 0)).astype(BF16)
    before = mm(lower, count.astype(BF16))
    rank = [jnp.sum(h * before, axis=1, keepdims=True) for h in hot]
    codes = [jnp.where(owner[k] >= 0, owner[k] * CAP + rank[k], -1.0) for k in range(3)]
    codes_p = (
        dev_id(lax.rem(x + 4 - r_a, 4), lax.rem(y + NY - r_y, NY), slot_b, lax.rem(c + NC - r_c, NC)) * CAP + slot_t
    ).astype(F32)

    def codes_q(dx):
        full = dev_id(lax.rem(x + dx, 4), lax.rem(y + r_y, NY), lax.rem(z + r_a, 4), lax.rem(c + r_c, NC)) * CAP + slot_t
        return jnp.where(slot_b == x, full, -2).astype(F32)

    def pick(code_row, values):
        total = jnp.zeros((ROWS, S), F32)
        for k in range(3):
            total = total + jnp.where(codes[k] == code_row, values[k], 0.0)
        return jnp.sum(total, axis=0, keepdims=True)

    w_row = pick(codes_p, hrow)
    query_number = iota((ROWS, 1), 0).astype(F32)
    query_and_row = [query_number + ROWS * hrow[k] for k in range(3)]
    pos_row = pos_ref[...].astype(F32)
    pos_wide = jnp.concatenate([pos_row] + [jnp.zeros((1, S - ROWS), F32)], axis=1)
    sub4 = iota((4, S), 0)
    for dx in range(4):
        table = jnp.where(
            sub4 == 0, pick(codes_q(dx), query_and_row), jnp.where(sub4 == 1, pos_wide, jnp.where(sub4 == 2, w_row, 0.0))
        )
        xt_s[dx] = table
        if dx == 0:
            xt_r[0] = table

    pl.semaphore_wait(barrier, 6 + YC - 1)
    p_in.wait()
    q_in.wait()

    def block(buf, i, col, width):
        return buf.at[pl.ds(lax.rem(i + 4, 4) * ROWS, ROWS), pl.ds(col, width)]

    def ring(which, kind, ch):
        buf, me = ((PZ, z), (QX, x))[which]
        step = 1 if kind in (0, 2) else 3
        blk = me if kind < 2 else (me - 1 if kind == 2 else me + 1)
        col = ch * DC + (H if kind == 3 else 0)
        width = DC if kind < 2 else H
        ref = block(buf, blk, col, width)
        target = dev(0, 0, step, 0) if which == 0 else dev(step, 0, 0, 0)
        return pltpu.make_async_remote_copy(
            ref, ref, ag_send.at[which, kind, ch], ag_recv.at[which, kind, ch],
            device_id=target, device_id_type=MESH,
        )

    def arriving(which, kind, ch):
        buf, me = ((PZ, z), (QX, x))[which]
        blk = (me - 1, me + 1, me - 2, me + 2)[kind]
        col = ch * DC + (H if kind == 3 else 0)
        width = DC if kind < 2 else H
        ref = block(buf, blk, col, width)
        return pltpu.make_async_remote_copy(
            ref, ref, ag_send.at[which, kind, ch], ag_recv.at[which, kind, ch],
            device_id=dev(0, 0, 1, 0), device_id_type=MESH,
        )

    def own_sends(ch):
        for which in (0, 1):
            ring(which, 0, ch).start()
            ring(which, 1, ch).start()

    def z_peer(dz):
        return pltpu.make_async_remote_copy(
            cz_s.at[0], cz_r.at[dz], cz_send.at[dz], cz_recv.at[dz], device_id=dev(0, 0, dz, 0), device_id_type=MESH
        )

    def yc_peer(kind, m):
        dy, dc = m // NC, m % NC
        if kind == 0:
            dy, dc = (NY - dy) % NY, (NC - dc) % NC
        src, dst = ((w_s, w_r), (c_s, c_r))[kind]
        return pltpu.make_async_remote_copy(
            src.at[0], dst.at[m], yc_send.at[kind], yc_recv.at[kind], device_id=dev(0, dy, 0, dc), device_id_type=MESH
        )

    def yc_all(kind):
        ref = (w_r, c_r)[kind].at[pl.ds(1, YC - 1)]
        return pltpu.make_async_remote_copy(
            ref, ref, yc_send.at[kind], yc_recv.at[kind], device_id=dev(1, 0, 0, 0), device_id_type=MESH
        )

    def fold(ref, group):
        values = ref[...]
        total = jnp.zeros(values.shape[1:], F32)
        for n in range(values.shape[0]):
            total = total + jnp.where(group == n, values[n], 0.0)
        return total

    def x_peer(src, dst, send, recv, dx):
        return pltpu.make_async_remote_copy(
            src.at[dx], dst.at[dx], send.at[dx], recv.at[dx], device_id=dev(dx, 0, 0, 0), device_id_type=MESH
        )

    def gather_matrix(index, slot):
        n = iota((S, 1), 0)
        want = to_column(index).astype(jnp.int32) + lax.rem(n, 16) // 4 * ROWS
        gather[slot] = (want == iota((S, 4 * ROWS), 1)).astype(BF16)

    def hard_starts(kind, ch):
        src, dst = ((SP, MP), (MQ, RQ))[kind]
        cols = pl.ds(ch * DC, DC)
        for m in SECOND[1:]:
            part = pl.ds(m * 16, 16)
            pltpu.make_async_remote_copy(
                src.at[:, part, cols], dst.at[:, part, cols], hard_send.at[kind, ch], hard_recv.at[kind, ch],
                device_id=dev(0, m // NC, 0, m % NC), device_id_type=MESH,
            ).start()
        dst[:, 0:16, cols] = src[:, 0:16, cols]

    def hard_all(kind, ch):
        ref = (MP, RQ)[kind].at[:, pl.ds(16, HR - 16), pl.ds(ch * DC, DC)]
        return pltpu.make_async_remote_copy(
            ref, ref, hard_send.at[kind, ch], hard_recv.at[kind, ch], device_id=dev(1, 0, 0, 0), device_id_type=MESH
        )

    def turn(kind, n, ch):
        cols = pl.ds(ch * DC, DC)
        src, dst = ((MP, RP), (SQ, MQ))[kind]
        return pltpu.make_async_remote_copy(
            src.at[n, :, cols], dst.at[n, :, cols], turn_send.at[kind, n, ch], turn_recv.at[kind, n, ch],
            device_id=dev(n, 0, 0, 0) if kind == 0 else dev(0, 0, n, 0), device_id_type=MESH,
        )

    def deliver(ch):
        cols = pl.ds(ch * DC, DC)
        hard_all(0, ch).wait_recv()
        for n in (1, 3, 2):
            turn(0, n, ch).start()
        RP[0, :, cols] = MP[0, :, cols]

    def second(ch):
        for n in range(1, 4):
            turn(1, n, ch).wait_recv()
        hard_starts(1, ch)

    def tiles(start, length, body):
        def step(t, carry):
            body(pl.ds(pl.multiple_of(start + t * TN, 128), TN))
            return carry

        lax.fori_loop(0, length // TN, step, 0)

    def serve_p(cols):
        rows = mm(gather[0], PZ[:, cols]).astype(BF16)
        for n in range(4):
            SP[n, :, cols] = rows[n * HR : (n + 1) * HR]

    def serve_q(cols):
        rows = mm(gather[1], QX[:, cols]).astype(BF16)
        for dz in range(4):
            (MQ if dz == 0 else SQ)[dz, :, cols] = rows[dz * HR : (dz + 1) * HR]

    me_rows = pl.ds(x * ROWS, ROWS)
    par_rows = pl.ds(lax.rem(x + 2, 4) * ROWS, ROWS)
    s_own[...] = jnp.zeros_like(s_own)
    s_par[...] = jnp.zeros_like(s_par)
    hs[...] = jnp.zeros_like(hs)

    def score(acc, rows, keys, ch):
        def body(cols):
            acc[...] += mm_t(QX[rows, cols], keys[:, cols])

        tiles(ch * DC, DC, body)

    def forward(ch):
        for which in (0, 1):
            for kind in (0, 1):
                arriving(which, kind, ch).wait_recv()
                ring(which, kind + 2, ch).start()

    own_sends(0)
    for dx in range(1, 4):
        x_peer(xt_s, xt_r, xt_send, xt_recv, dx).start()
    own_sends(1)
    for dx in range(1, 4):
        x_peer(xt_s, xt_r, xt_send, xt_recv, dx).wait_recv()
    tables = (xt_r[0] + xt_r[1] + xt_r[2] + xt_r[3])[0:1, :].astype(jnp.int32)
    wanted = jnp.zeros((1, S), F32)
    for dx in range(4):
        wanted = wanted + jnp.where(r_a == (4 - dx) % 4, xt_r[dx][2:3, :], 0.0)
    w_s[0] = wanted
    w_r[0] = wanted
    for m in range(1, YC):
        yc_peer(0, m).start()
    j_all = (tables // ROWS).astype(F32)
    forward(0)
    own_sends(2)
    gather_matrix(lax.rem(tables, ROWS).astype(F32), 1)
    yc_all(0).wait_recv()
    gather_matrix(fold(w_r, r_y * NC + r_c), 0)

    for ch in range(NCH):
        if ch + 1 < NCH:
            forward(ch + 1)
        if ch + 3 < NCH:
            own_sends(ch + 3)
        arriving(0, 2, ch).wait_recv()
        arriving(0, 3, ch).wait_recv()
        tiles(ch * DC, DC, serve_p)
        hard_starts(0, ch)
        if ch > 0:
            deliver(ch - 1)
        arriving(1, 2, ch).wait_recv()
        arriving(1, 3, ch).wait_recv()
        tiles(ch * DC, DC, serve_q)
        for dz in (1, 3, 2):
            turn(1, dz, ch).start()
        score(s_own, me_rows, PZ, ch)
        score(s_par, par_rows, PZ, ch)
    deliver(NCH - 1)

    def hard_score(cols):
        hs[...] += mm_t(QX[me_rows, cols], RP[:, :, cols].reshape(S, TN))

    base = (xh * 4 * ROWS).astype(F32)
    lane_p = iota((ROWS, 4 * ROWS), 1).astype(F32)
    pos_own = to_column(pos_row) - base
    pos_par = to_column(xt_r[2][1:2, 0:ROWS]) - base

    def half_stats(acc, pos):
        s = acc[...] * LOGIT_SCALE
        m = jnp.max(s, axis=1, keepdims=True)
        l = jnp.sum(jnp.exp(s - m), axis=1, keepdims=True)
        sp = jnp.sum(jnp.where(lane_p == pos, s, 0.0), axis=1, keepdims=True)
        return m, l, sp

    lane128 = iota((ROWS, 128), 1)
    m_p, l_p, sp_p = half_stats(s_par, pos_par)
    st_s[...] = jnp.where(lane128 == 0, m_p, jnp.where(lane128 == 1, l_p, jnp.where(lane128 == 2, sp_p, 0.0)))

    def pair(src, dst, i):
        return pltpu.make_async_remote_copy(
            src, dst, pair_send.at[i], pair_recv.at[i], device_id=dev(2, 0, 0, 0), device_id_type=MESH
        )

    pair(st_s, st_r, 0).start()
    m_o, l_o, sp_o = half_stats(s_own, pos_own)

    for ch in range(NCH):
        for n in range(1, 4):
            turn(0, n, ch).wait_recv()
        tiles(ch * DC, DC, hard_score)
        if ch in EARLY:
            second(EARLY.index(ch))
    pair(st_s, st_r, 0).wait_recv()
    stats = st_r[...]
    m_r, l_r, sp_r = stats[:, 0:1], stats[:, 1:2], stats[:, 2:3]
    scaled = hs[...] * LOGIT_SCALE + shift
    mask = [codes[k] == codes_p for k in range(3)]
    hard_k = [jnp.sum(jnp.where(mask[k], scaled, 0.0), axis=1, keepdims=True) for k in range(3)]
    present = [jnp.where(owner[k] >= 0, hard_k[k], NEG) for k in range(3)]
    top = jnp.maximum(jnp.maximum(m_o, m_r), jnp.maximum(jnp.maximum(present[0], present[1]), present[2]))
    total = l_o * jnp.exp(m_o - top) + l_r * jnp.exp(m_r - top)
    for k in range(3):
        total = total + jnp.exp(present[k] - top)
    lse = top + jnp.log(total)
    lse_s[...] = jnp.broadcast_to(lse, (ROWS, 128))
    pair(lse_s, lse_r, 1).start()
    loss_ref[...] = to_row(lse - (sp_o + sp_r))
    hard_coef = [jnp.exp(present[k] - lse) for k in range(3)]

    def half_coef(acc, pos, row_lse, out, column):
        f = jnp.exp(acc[...] * LOGIT_SCALE - row_lse) - jnp.where(lane_p == pos, 1.0, 0.0)
        out[...] = f.astype(BF16)
        coef_t[:, column * ROWS : (column + 1) * ROWS] = jnp.transpose(f).astype(BF16)

    half_coef(s_own, pos_own, lse, coef_o, 0)
    pair(lse_s, lse_r, 1).wait_recv()
    half_coef(s_par, pos_par, lse_r[:, 0:1], coef_p, 1)

    def passage_part(offset, cols):
        ct = coef_t[pl.ds(lax.rem(z + offset, 4) * ROWS, ROWS), :]
        part = mm(ct[:, 0:ROWS], QX[me_rows, cols]) + mm(ct[:, ROWS : 2 * ROWS], QX[par_rows, cols])
        return part * LOGIT_SCALE

    def rs(src, dst, i, step, start, length):
        return pltpu.make_async_remote_copy(
            src.at[:, pl.ds(start, length)], dst.at[:, pl.ds(start, length)], rs_send.at[i], rs_recv.at[i],
            device_id=dev(0, 0, step, 0), device_id_type=MESH,
        )

    far_up = rs(rs_a, rr_a, 0, 1, 0, HD)
    far_dn = rs(rs_a, rr_a, 1, 3, HD, HD)
    up_free = rs(rs_up, rr_up, 2, 1, HD, HD)
    dn_free = rs(rs_dn, rr_dn, 3, 3, 0, HD)
    up_last = rs(rs_up, rr_up, 4, 1, 0, HD)
    dn_last = rs(rs_dn, rr_dn, 5, 3, HD, HD)

    def far(cols):
        rs_a[:, cols] = passage_part(2, cols).astype(BF16)

    tiles(0, HD, far)
    far_up.start()
    tiles(HD, HD, far)
    far_dn.start()

    for dx in range(4):
        row = pick(codes_q(dx), hard_coef)
        cx_s[dx] = row
        if dx == 0:
            cx_r[0] = row
    for dx in range(1, 4):
        x_peer(cx_s, cx_r, cx_send, cx_recv, dx).start()

    def partner_part(cols):
        gx_s[:, cols] = (mm(coef_p[...], PZ[:, cols]) * LOGIT_SCALE).astype(BF16)

    tiles(0, D, partner_part)
    pair(gx_s, gx_r, 2).start()

    def up_part(cols):
        rs_up[:, cols] = passage_part(1, cols).astype(BF16)

    def dn_part(cols):
        rs_dn[:, cols] = passage_part(3, cols).astype(BF16)

    tiles(HD, HD, up_part)
    up_free.start()
    tiles(0, HD, dn_part)
    dn_free.start()

    for dx in range(1, 4):
        x_peer(cx_s, cx_r, cx_send, cx_recv, dx).wait_recv()
    both = jnp.where(iota((2, S), 0) == 0, cx_r[0] + cx_r[1] + cx_r[2] + cx_r[3], j_all)
    cz_s[0] = both
    cz_r[0] = both
    for dz in (1, 3, 2):
        z_peer(dz).start()
    for ch in range(len(EARLY), NCH):
        second(ch)

    far_up.wait_recv()

    def up_sum(cols):
        rs_up[:, cols] = (passage_part(1, cols) + rr_a[:, cols].astype(F32)).astype(BF16)

    tiles(0, HD, up_sum)
    up_last.start()
    far_dn.wait_recv()

    def dn_sum(cols):
        rs_dn[:, cols] = (passage_part(3, cols) + rr_a[:, cols].astype(F32)).astype(BF16)

    tiles(HD, HD, dn_sum)
    dn_last.start()

    for dz in range(1, 4):
        z_peer(dz).wait_recv()
    both = fold(cz_r, r_a)
    c_s[0] = both
    c_r[0] = both
    for m in range(1, YC):
        yc_peer(1, m).start()

    h = jnp.zeros((ROWS, S), F32)
    for k in range(3):
        h = h + jnp.where(mask[k], hard_coef[k], 0.0)
    hmat[...] = h.astype(BF16)
    pair(gx_s, gx_r, 2).wait_recv()

    def query_grad(cols):
        part = mm(coef_o[...], PZ[:, cols]) + mm(hmat[...], RP[:, :, cols].reshape(S, TN))
        gq_ref[:, cols] = part * LOGIT_SCALE + gx_r[:, cols].astype(F32)

    tiles(0, D, query_grad)
    gq_out = pltpu.make_async_copy(gq_ref, gq_hbm, out_sem.at[0])
    gq_out.start()

    yc_all(1).wait_recv()
    both = fold(c_r, r_y * NC + r_c)
    hmat[...] = jnp.where(query_number == both[1:2, :], both[0:1, :], 0.0).astype(BF16)
    for ch in range(NCH):
        hard_all(1, ch).wait_recv()

        def passage_grad(cols):
            gp_ref[:, cols] = passage_part(0, cols) + LOGIT_SCALE * mm(hmat[...], RQ[:, :, cols].reshape(S, TN))

        tiles(ch * DC, DC, passage_grad)
    up_free.wait_recv()
    dn_free.wait_recv()
    up_last.wait_recv()
    dn_last.wait_recv()

    def last(cols):
        gp_ref[:, cols] += rr_up[:, cols].astype(F32) + rr_dn[:, cols].astype(F32)

    outs = [gq_out]
    for ch in range(4):
        tiles(ch * D // 4, D // 4, last)
        cols = pl.ds(ch * D // 4, D // 4)
        outs.append(pltpu.make_async_copy(gp_ref.at[:, cols], gp_hbm.at[:, cols], out_sem.at[1 + ch]))
        outs[-1].start()

    for ch in range(NCH):
        for which in (0, 1):
            for kind in range(4):
                ring(which, kind, ch).wait_send()
            hard_all(which, ch).wait_send()
        for n in range(1, 4):
            turn(0, n, ch).wait_send()
            turn(1, n, ch).wait_send()
    for dx in range(1, 4):
        x_peer(xt_s, xt_r, xt_send, xt_recv, dx).wait_send()
        x_peer(cx_s, cx_r, cx_send, cx_recv, dx).wait_send()
    for dz in range(1, 4):
        z_peer(dz).wait_send()
    yc_all(0).wait_send()
    yc_all(1).wait_send()
    pair(st_s, st_r, 0).wait_send()
    pair(lse_s, lse_r, 1).wait_send()
    pair(gx_s, gx_r, 2).wait_send()
    for copy in (far_up, far_dn, up_free, dn_free, up_last, dn_last):
        copy.wait_send()
    for copy in outs:
        copy.wait()


def results(loss_in, gq_in, gp_in, loss_out, gq_out, gp_out):
    loss_out[...] = loss_in[...]
    gq_out[...] = gq_in[...]
    gp_out[...] = gp_in[...]


def on_device(ngrp, queries, passages, positives, hard_owner, hard_row):
    D = queries.shape[1]
    NC = 2 if ngrp % 4 == 0 else 1
    NY = ngrp // (2 * NC)
    R = 4 * NY * NC
    S = 16 * R
    shift = math.log(8 * ROWS / 3)
    vmem = pltpu.VMEM
    dma = pltpu.SemaphoreType.DMA
    wide = vmem((ROWS, D), BF16)
    parts = vmem((4, S // 4, D), BF16)
    any_spec = pl.BlockSpec(memory_space=pl.ANY)
    vmem_spec = pl.BlockSpec(memory_space=pltpu.VMEM)
    loss, gq, gp = pl.pallas_call(
        functools.partial(kernel, NY, NC, D, shift),
        out_shape=(
            jax.ShapeDtypeStruct((1, ROWS), F32),
            jax.ShapeDtypeStruct((ROWS, D), F32),
            jax.ShapeDtypeStruct((ROWS, D), F32),
        ),
        in_specs=[any_spec, any_spec, vmem_spec, vmem_spec, vmem_spec],
        out_specs=(vmem_spec, any_spec, any_spec),
        scratch_shapes=[
            vmem((4 * ROWS, D), BF16), vmem((4 * ROWS, D), BF16),
            parts, parts, parts, parts, parts, parts,
            wide, wide, wide, wide, wide, wide, wide, wide,
            vmem((ROWS, 4 * ROWS), F32), vmem((ROWS, 4 * ROWS), F32), vmem((ROWS, S), F32),
            vmem((2, S, 4 * ROWS), BF16),
            vmem((ROWS, 4 * ROWS), BF16), vmem((ROWS, 4 * ROWS), BF16), vmem((4 * ROWS, 2 * ROWS), BF16),
            vmem((ROWS, S), BF16),
            vmem((4, 4, S), F32), vmem((4, 4, S), F32),
            vmem((1, 1, S), F32), vmem((NY * NC, 1, S), F32),
            vmem((4, 1, S), F32), vmem((4, 1, S), F32),
            vmem((1, 2, S), F32), vmem((4, 2, S), F32),
            vmem((1, 2, S), F32), vmem((NY * NC, 2, S), F32),
            vmem((ROWS, 128), F32), vmem((ROWS, 128), F32), vmem((ROWS, 128), F32), vmem((ROWS, 128), F32),
            vmem((ROWS, D), F32), vmem((ROWS, D), F32),
            dma((2,)), dma((5,)), dma((2, 4, NCH)), dma((2, 4, NCH)), dma((2, NCH)), dma((2, NCH)),
            dma((4,)), dma((4,)), dma((4,)), dma((4,)), dma((4,)), dma((4,)), dma((2, 4, NCH)), dma((2, 4, NCH)), dma((2,)), dma((2,)), dma((3,)), dma((3,)),
            dma((6,)), dma((6,)),
        ],
        compiler_params=pltpu.CompilerParams(
            collective_id=0, has_side_effects=True, vmem_limit_bytes=60 * 2**20
        ),
        cost_estimate=pl.CostEstimate(flops=9 * 10**9, bytes_accessed=8 * 2**20, transcendentals=2 * 10**5),
        name="infonce",
    )(queries, passages, positives, hard_owner.T, hard_row.T)
    block = pl.BlockSpec((ROWS // 2, D), lambda i: (i, 0))
    row = pl.BlockSpec((1, ROWS), lambda i: (0, 0))
    loss, gq, gp = pl.pallas_call(
        results,
        grid=(2,),
        in_specs=[row, block, block],
        out_specs=(row, block, block),
        out_shape=tuple(jax.ShapeDtypeStruct(a.shape, F32) for a in (loss, gq, gp)),
        name="results",
    )(loss, gq, gp)
    return loss.reshape(ROWS), gq, gp


def solution(mesh):
    return jax.shard_map(
        functools.partial(on_device, mesh.shape["grp"]),
        mesh=mesh,
        in_specs=(
            P(("grp", "blk"), None),
            P(("grp", "blk"), None),
            P("grp", "blk"),
            P(("grp", "blk"), None),
            P(("grp", "blk"), None),
        ),
        out_specs=(P(("grp", "blk")), P(("grp", "blk"), None), P(("grp", "blk"), None)),
        check_vma=False,
    )
```

```python
import functools
import math

import jax
import jax.numpy as jnp
from jax import lax
from jax.experimental import pallas as pl
from jax.experimental.pallas import tpu as pltpu
from jax.sharding import PartitionSpec as P

LOGIT_SCALE = 20.0
ROWS = 128
CAP = 4
NCH = 4
EARLY = (1, 2, 3)
NEG = -1e30
MESH = pl.DeviceIdType.MESH
F32 = jnp.float32
BF16 = jnp.bfloat16


def iota(shape, dim):
    return lax.broadcasted_iota(jnp.int32, shape, dim)


def to_column(row):
    n = row.shape[1]
    eye = iota((n, n), 0) == iota((n, n), 1)
    return jnp.sum(jnp.where(eye, row, jnp.zeros_like(row)), axis=1, keepdims=True)


def to_row(col):
    n = col.shape[0]
    eye = iota((n, n), 0) == iota((n, n), 1)
    return jnp.sum(jnp.where(eye, col, jnp.zeros_like(col)), axis=0, keepdims=True)


def mm(a, b):
    return jnp.dot(a, b, preferred_element_type=F32)


def mm_t(a, b):
    return lax.dot_general(a, b, (((1,), (1,)), ((), ())), preferred_element_type=F32)


def kernel(
    NY, NC, D, shift,
    q_hbm, p_hbm, pos_ref, own_ref, row_ref,
    loss_ref, gq_hbm, gp_hbm, rr_up, rr_dn, gx_r,
    PZ, QX, SP, SQ, MP, RP, MQ, RQ,
    rs_a, rs_up, rs_dn, rr_a, gx_s,
    s_own, s_par, hs, gather, coef_o, coef_p, coef_t, hmat,
    xt_s, xt_r, w_s, w_r, cx_s, cx_r, cz_s, cz_r, c_s, c_r, st_s, st_r, lse_s, lse_r, gq_ref, gp_ref,
    in_sem, out_sem, ag_send, ag_recv, hard_send, hard_recv,
    xt_send, xt_recv, cx_send, cx_recv, cz_send, cz_recv, turn_send, turn_recv, yc_send, yc_recv, pair_send, pair_recv, rs_send, rs_recv,
):
    R = 4 * NY * NC
    S = 16 * R
    YC = NY * NC
    HR = S // 4
    SECOND = [0] + sorted(range(1, NY * NC), key=lambda m: (m % NC, m // NC == 2, m))
    DC = D // NCH
    H = DC // 2
    HD = D // 2
    TN = min(512, H)
    g = lax.axis_index("grp")
    b = lax.axis_index("blk")
    z = lax.rem(b, 4)
    xh = b // 4
    c = lax.rem(g, NC)
    x = xh * 2 + lax.rem(g // NC, 2)
    y = g // (2 * NC)

    def dev(dx, dy, dz, dc):
        x2 = lax.rem(x + dx, 4)
        y2 = lax.rem(y + dy, NY)
        z2 = lax.rem(z + dz, 4)
        c2 = lax.rem(c + dc, NC)
        return ((y2 * 2 + lax.rem(x2, 2)) * NC + c2, (x2 // 2) * 4 + z2)

    p_in = pltpu.make_async_copy(p_hbm, PZ.at[pl.ds(z * ROWS, ROWS)], in_sem.at[0])
    q_in = pltpu.make_async_copy(q_hbm, QX.at[pl.ds(x * ROWS, ROWS)], in_sem.at[1])
    p_in.start()
    q_in.start()
    barrier = pltpu.get_barrier_semaphore()

    for n in range(1, 4):
        pl.semaphore_signal(barrier, inc=1, device_id=dev(n, 0, 0, 0), device_id_type=MESH)
        pl.semaphore_signal(barrier, inc=1, device_id=dev(0, 0, n, 0), device_id_type=MESH)
    for m in range(1, YC):
        pl.semaphore_signal(barrier, inc=1, device_id=dev(0, m // NC, 0, m % NC), device_id_type=MESH)
    lane = iota((1, S), 1)
    slot_r = lane // 16
    slot_b = lax.rem(lane, 16) // 4
    slot_t = lax.rem(lane, 4)
    r_a = slot_r // (NY * NC)
    r_y = lax.rem(slot_r // NC, NY)
    r_c = lax.rem(slot_r, NC)

    def dev_id(x2, y2, z2, c2):
        return ((y2 * 2 + lax.rem(x2, 2)) * NC + c2) * 8 + (x2 // 2) * 4 + z2

    owner = [to_column(own_ref[k : k + 1, :].astype(F32)) for k in range(3)]
    hrow = [to_column(row_ref[k : k + 1, :].astype(F32)) for k in range(3)]
    ndev = 8 * 2 * NY * NC
    lane_o = iota((ROWS, max(ndev, 128)), 1).astype(F32)
    hot = [(owner[k] == lane_o).astype(F32) for k in range(3)]
    count = hot[0] + hot[1] + hot[2]
    lower = (iota((ROWS, ROWS), 1) < iota((ROWS, ROWS), 0)).astype(BF16)
    before = mm(lower, count.astype(BF16))
    rank = [jnp.sum(h * before, axis=1, keepdims=True) for h in hot]
    codes = [jnp.where(owner[k] >= 0, owner[k] * CAP + rank[k], -1.0) for k in range(3)]
    codes_p = (
        dev_id(lax.rem(x + 4 - r_a, 4), lax.rem(y + NY - r_y, NY), slot_b, lax.rem(c + NC - r_c, NC)) * CAP + slot_t
    ).astype(F32)

    def codes_q(dx):
        full = dev_id(lax.rem(x + dx, 4), lax.rem(y + r_y, NY), lax.rem(z + r_a, 4), lax.rem(c + r_c, NC)) * CAP + slot_t
        return jnp.where(slot_b == x, full, -2).astype(F32)

    def pick(code_row, values):
        total = jnp.zeros((ROWS, S), F32)
        for k in range(3):
            total = total + jnp.where(codes[k] == code_row, values[k], 0.0)
        return jnp.sum(total, axis=0, keepdims=True)

    w_row = pick(codes_p, hrow)
    query_number = iota((ROWS, 1), 0).astype(F32)
    query_and_row = [query_number + ROWS * hrow[k] for k in range(3)]
    pos_row = pos_ref[...].astype(F32)
    pos_wide = jnp.concatenate([pos_row] + [jnp.zeros((1, S - ROWS), F32)], axis=1)
    sub4 = iota((4, S), 0)
    for dx in range(4):
        table = jnp.where(
            sub4 == 0, pick(codes_q(dx), query_and_row), jnp.where(sub4 == 1, pos_wide, jnp.where(sub4 == 2, w_row, 0.0))
        )
        xt_s[dx] = table
        if dx == 0:
            xt_r[0] = table

    pl.semaphore_wait(barrier, 6 + YC - 1)
    p_in.wait()
    q_in.wait()

    def block(buf, i, col, width):
        return buf.at[pl.ds(lax.rem(i + 4, 4) * ROWS, ROWS), pl.ds(col, width)]

    def ring(which, kind, ch):
        buf, me = ((PZ, z), (QX, x))[which]
        step = 1 if kind in (0, 2) else 3
        blk = me if kind < 2 else (me - 1 if kind == 2 else me + 1)
        col = ch * DC + (H if kind == 3 else 0)
        width = DC if kind < 2 else H
        ref = block(buf, blk, col, width)
        target = dev(0, 0, step, 0) if which == 0 else dev(step, 0, 0, 0)
        return pltpu.make_async_remote_copy(
            ref, ref, ag_send.at[which, kind, ch], ag_recv.at[which, kind, ch],
            device_id=target, device_id_type=MESH,
        )

    def arriving(which, kind, ch):
        buf, me = ((PZ, z), (QX, x))[which]
        blk = (me - 1, me + 1, me - 2, me + 2)[kind]
        col = ch * DC + (H if kind == 3 else 0)
        width = DC if kind < 2 else H
        ref = block(buf, blk, col, width)
        return pltpu.make_async_remote_copy(
            ref, ref, ag_send.at[which, kind, ch], ag_recv.at[which, kind, ch],
            device_id=dev(0, 0, 1, 0), device_id_type=MESH,
        )

    def own_sends(ch):
        for which in (0, 1):
            ring(which, 0, ch).start()
            ring(which, 1, ch).start()

    def z_peer(dz):
        return pltpu.make_async_remote_copy(
            cz_s.at[0], cz_r.at[dz], cz_send.at[dz], cz_recv.at[dz], device_id=dev(0, 0, dz, 0), device_id_type=MESH
        )

    def yc_peer(kind, m):
        dy, dc = m // NC, m % NC
        if kind == 0:
            dy, dc = (NY - dy) % NY, (NC - dc) % NC
        src, dst = ((w_s, w_r), (c_s, c_r))[kind]
        return pltpu.make_async_remote_copy(
            src.at[0], dst.at[m], yc_send.at[kind], yc_recv.at[kind], device_id=dev(0, dy, 0, dc), device_id_type=MESH
        )

    def yc_all(kind):
        ref = (w_r, c_r)[kind].at[pl.ds(1, YC - 1)]
        return pltpu.make_async_remote_copy(
            ref, ref, yc_send.at[kind], yc_recv.at[kind], device_id=dev(1, 0, 0, 0), device_id_type=MESH
        )

    def fold(ref, group):
        values = ref[...]
        total = jnp.zeros(values.shape[1:], F32)
        for n in range(values.shape[0]):
            total = total + jnp.where(group == n, values[n], 0.0)
        return total

    def x_peer(src, dst, send, recv, dx):
        return pltpu.make_async_remote_copy(
            src.at[dx], dst.at[dx], send.at[dx], recv.at[dx], device_id=dev(dx, 0, 0, 0), device_id_type=MESH
        )

    def gather_matrix(index, slot):
        n = iota((S, 1), 0)
        want = to_column(index).astype(jnp.int32) + lax.rem(n, 16) // 4 * ROWS
        gather[slot] = (want == iota((S, 4 * ROWS), 1)).astype(BF16)

    def hard_starts(kind, ch):
        src, dst = ((SP, MP), (MQ, RQ))[kind]
        cols = pl.ds(ch * DC, DC)
        for m in SECOND[1:]:
            part = pl.ds(m * 16, 16)
            pltpu.make_async_remote_copy(
                src.at[:, part, cols], dst.at[:, part, cols], hard_send.at[kind, ch], hard_recv.at[kind, ch],
                device_id=dev(0, m // NC, 0, m % NC), device_id_type=MESH,
            ).start()
        dst[:, 0:16, cols] = src[:, 0:16, cols]

    def hard_all(kind, ch):
        ref = (MP, RQ)[kind].at[:, pl.ds(16, HR - 16), pl.ds(ch * DC, DC)]
        return pltpu.make_async_remote_copy(
            ref, ref, hard_send.at[kind, ch], hard_recv.at[kind, ch], device_id=dev(1, 0, 0, 0), device_id_type=MESH
        )

    def turn(kind, n, ch):
        cols = pl.ds(ch * DC, DC)
        src, dst = ((MP, RP), (SQ, MQ))[kind]
        return pltpu.make_async_remote_copy(
            src.at[n, :, cols], dst.at[n, :, cols], turn_send.at[kind, n, ch], turn_recv.at[kind, n, ch],
            device_id=dev(n, 0, 0, 0) if kind == 0 else dev(0, 0, n, 0), device_id_type=MESH,
        )

    def deliver(ch):
        cols = pl.ds(ch * DC, DC)
        hard_all(0, ch).wait_recv()
        for n in (1, 3, 2):
            turn(0, n, ch).start()
        RP[0, :, cols] = MP[0, :, cols]

    def second(ch):
        for n in range(1, 4):
            turn(1, n, ch).wait_recv()
        hard_starts(1, ch)

    def tiles(start, length, body):
        def step(t, carry):
            body(pl.ds(pl.multiple_of(start + t * TN, 128), TN))
            return carry

        lax.fori_loop(0, length // TN, step, 0)

    def serve_p(cols):
        rows = mm(gather[0], PZ[:, cols]).astype(BF16)
        for n in range(4):
            SP[n, :, cols] = rows[n * HR : (n + 1) * HR]

    def serve_q(cols):
        rows = mm(gather[1], QX[:, cols]).astype(BF16)
        for dz in range(4):
            (MQ if dz == 0 else SQ)[dz, :, cols] = rows[dz * HR : (dz + 1) * HR]

    me_rows = pl.ds(x * ROWS, ROWS)
    par_rows = pl.ds(lax.rem(x + 2, 4) * ROWS, ROWS)
    s_own[...] = jnp.zeros_like(s_own)
    s_par[...] = jnp.zeros_like(s_par)
    hs[...] = jnp.zeros_like(hs)

    def score(acc, rows, keys, ch):
        def body(cols):
            acc[...] += mm_t(QX[rows, cols], keys[:, cols])

        tiles(ch * DC, DC, body)

    def forward(ch):
        for which in (0, 1):
            for kind in (0, 1):
                arriving(which, kind, ch).wait_recv()
                ring(which, kind + 2, ch).start()

    own_sends(0)
    for dx in range(1, 4):
        x_peer(xt_s, xt_r, xt_send, xt_recv, dx).start()
    own_sends(1)
    for dx in range(1, 4):
        x_peer(xt_s, xt_r, xt_send, xt_recv, dx).wait_recv()
    tables = (xt_r[0] + xt_r[1] + xt_r[2] + xt_r[3])[0:1, :].astype(jnp.int32)
    wanted = jnp.zeros((1, S), F32)
    for dx in range(4):
        wanted = wanted + jnp.where(r_a == (4 - dx) % 4, xt_r[dx][2:3, :], 0.0)
    w_s[0] = wanted
    w_r[0] = wanted
    for m in range(1, YC):
        yc_peer(0, m).start()
    j_all = (tables // ROWS).astype(F32)
    forward(0)
    own_sends(2)
    gather_matrix(lax.rem(tables, ROWS).astype(F32), 1)
    yc_all(0).wait_recv()
    gather_matrix(fold(w_r, r_y * NC + r_c), 0)

    for ch in range(NCH):
        if ch + 1 < NCH:
            forward(ch + 1)
        if ch + 3 < NCH:
            own_sends(ch + 3)
        arriving(0, 2, ch).wait_recv()
        arriving(0, 3, ch).wait_recv()
        tiles(ch * DC, DC, serve_p)
        hard_starts(0, ch)
        if ch > 0:
            deliver(ch - 1)
        arriving(1, 2, ch).wait_recv()
        arriving(1, 3, ch).wait_recv()
        tiles(ch * DC, DC, serve_q)
        for dz in (1, 3, 2):
            turn(1, dz, ch).start()
        score(s_own, me_rows, PZ, ch)
        score(s_par, par_rows, PZ, ch)
    deliver(NCH - 1)

    def hard_score(cols):
        hs[...] += mm_t(QX[me_rows, cols], RP[:, :, cols].reshape(S, TN))

    base = (xh * 4 * ROWS).astype(F32)
    lane_p = iota((ROWS, 4 * ROWS), 1).astype(F32)
    pos_own = to_column(pos_row) - base
    pos_par = to_column(xt_r[2][1:2, 0:ROWS]) - base

    def half_stats(acc, pos):
        s = acc[...] * LOGIT_SCALE
        m = jnp.max(s, axis=1, keepdims=True)
        l = jnp.sum(jnp.exp(s - m), axis=1, keepdims=True)
        sp = jnp.sum(jnp.where(lane_p == pos, s, 0.0), axis=1, keepdims=True)
        return m, l, sp

    lane128 = iota((ROWS, 128), 1)
    m_p, l_p, sp_p = half_stats(s_par, pos_par)
    st_s[...] = jnp.where(lane128 == 0, m_p, jnp.where(lane128 == 1, l_p, jnp.where(lane128 == 2, sp_p, 0.0)))

    def pair(src, dst, i):
        return pltpu.make_async_remote_copy(
            src, dst, pair_send.at[i], pair_recv.at[i], device_id=dev(2, 0, 0, 0), device_id_type=MESH
        )

    pair(st_s, st_r, 0).start()
    m_o, l_o, sp_o = half_stats(s_own, pos_own)

    for ch in range(NCH):
        for n in range(1, 4):
            turn(0, n, ch).wait_recv()
        tiles(ch * DC, DC, hard_score)
        if ch in EARLY:
            second(EARLY.index(ch))
    pair(st_s, st_r, 0).wait_recv()
    stats = st_r[...]
    m_r, l_r, sp_r = stats[:, 0:1], stats[:, 1:2], stats[:, 2:3]
    scaled = hs[...] * LOGIT_SCALE + shift
    mask = [codes[k] == codes_p for k in range(3)]
    hard_k = [jnp.sum(jnp.where(mask[k], scaled, 0.0), axis=1, keepdims=True) for k in range(3)]
    present = [jnp.where(owner[k] >= 0, hard_k[k], NEG) for k in range(3)]
    top = jnp.maximum(jnp.maximum(m_o, m_r), jnp.maximum(jnp.maximum(present[0], present[1]), present[2]))
    total = l_o * jnp.exp(m_o - top) + l_r * jnp.exp(m_r - top)
    for k in range(3):
        total = total + jnp.exp(present[k] - top)
    lse = top + jnp.log(total)
    lse_s[...] = jnp.broadcast_to(lse, (ROWS, 128))
    pair(lse_s, lse_r, 1).start()
    loss_ref[...] = to_row(lse - (sp_o + sp_r))
    hard_coef = [jnp.exp(present[k] - lse) for k in range(3)]

    for dx in range(4):
        row = pick(codes_q(dx), hard_coef)
        cx_s[dx] = row
        if dx == 0:
            cx_r[0] = row
    for dx in range(1, 4):
        x_peer(cx_s, cx_r, cx_send, cx_recv, dx).start()

    def half_coef(acc, pos, row_lse, out, column):
        f = jnp.exp(acc[...] * LOGIT_SCALE - row_lse) - jnp.where(lane_p == pos, 1.0, 0.0)
        out[...] = f.astype(BF16)
        coef_t[:, column * ROWS : (column + 1) * ROWS] = jnp.transpose(f).astype(BF16)

    half_coef(s_own, pos_own, lse, coef_o, 0)
    pair(lse_s, lse_r, 1).wait_recv()
    half_coef(s_par, pos_par, lse_r[:, 0:1], coef_p, 1)

    def passage_part(offset, cols):
        ct = coef_t[pl.ds(lax.rem(z + offset, 4) * ROWS, ROWS), :]
        part = mm(ct[:, 0:ROWS], QX[me_rows, cols]) + mm(ct[:, ROWS : 2 * ROWS], QX[par_rows, cols])
        return part * LOGIT_SCALE

    def rs(src, dst, i, step, start, length):
        return pltpu.make_async_remote_copy(
            src.at[:, pl.ds(start, length)], dst.at[:, pl.ds(start, length)], rs_send.at[i], rs_recv.at[i],
            device_id=dev(0, 0, step, 0), device_id_type=MESH,
        )

    far_up = rs(rs_a, rr_a, 0, 1, 0, HD)
    far_dn = rs(rs_a, rr_a, 1, 3, HD, HD)
    up_free = rs(rs_up, rr_up, 2, 1, HD, HD)
    dn_free = rs(rs_dn, rr_dn, 3, 3, 0, HD)
    up_last = rs(rs_up, rr_up, 4, 1, 0, HD)
    dn_last = rs(rs_dn, rr_dn, 5, 3, HD, HD)

    def far(cols):
        rs_a[:, cols] = passage_part(2, cols).astype(BF16)

    for dx in range(1, 4):
        x_peer(cx_s, cx_r, cx_send, cx_recv, dx).wait_recv()
    both = jnp.where(iota((2, S), 0) == 0, cx_r[0] + cx_r[1] + cx_r[2] + cx_r[3], j_all)
    cz_s[0] = both
    cz_r[0] = both
    for dz in (1, 3, 2):
        z_peer(dz).start()
    tiles(0, HD, far)
    far_up.start()
    tiles(HD, HD, far)
    far_dn.start()

    def partner_part(cols):
        gx_s[:, cols] = (mm(coef_p[...], PZ[:, cols]) * LOGIT_SCALE).astype(BF16)

    tiles(0, D, partner_part)
    pair(gx_s, gx_r, 2).start()

    def up_part(cols):
        rs_up[:, cols] = passage_part(1, cols).astype(BF16)

    def dn_part(cols):
        rs_dn[:, cols] = passage_part(3, cols).astype(BF16)

    for dz in range(1, 4):
        z_peer(dz).wait_recv()
    both = fold(cz_r, r_a)
    c_s[0] = both
    c_r[0] = both
    for m in range(1, YC):
        yc_peer(1, m).start()

    tiles(HD, HD, up_part)
    up_free.start()
    tiles(0, HD, dn_part)
    dn_free.start()

    for ch in range(len(EARLY), NCH):
        second(ch)

    far_up.wait_recv()

    def up_sum(cols):
        rs_up[:, cols] = (passage_part(1, cols) + rr_a[:, cols].astype(F32)).astype(BF16)

    tiles(0, HD, up_sum)
    up_last.start()
    far_dn.wait_recv()

    def dn_sum(cols):
        rs_dn[:, cols] = (passage_part(3, cols) + rr_a[:, cols].astype(F32)).astype(BF16)

    tiles(HD, HD, dn_sum)
    dn_last.start()

    h = jnp.zeros((ROWS, S), F32)
    for k in range(3):
        h = h + jnp.where(mask[k], hard_coef[k], 0.0)
    hmat[...] = h.astype(BF16)

    def query_grad(cols):
        part = mm(coef_o[...], PZ[:, cols]) + mm(hmat[...], RP[:, :, cols].reshape(S, TN))
        gq_ref[:, cols] = (part * LOGIT_SCALE).astype(BF16)

    tiles(0, D, query_grad)
    gq_out = pltpu.make_async_copy(gq_ref, gq_hbm, out_sem.at[0])
    gq_out.start()

    yc_all(1).wait_recv()
    both = fold(c_r, r_y * NC + r_c)
    hmat[...] = jnp.where(query_number == both[1:2, :], both[0:1, :], 0.0).astype(BF16)
    for ch in range(NCH):
        hard_all(1, ch).wait_recv()

        def passage_grad(cols):
            total = passage_part(0, cols) + LOGIT_SCALE * mm(hmat[...], RQ[:, :, cols].reshape(S, TN))
            gp_ref[:, cols] = total.astype(BF16)

        tiles(ch * DC, DC, passage_grad)
    gp_out = pltpu.make_async_copy(gp_ref, gp_hbm, out_sem.at[1])
    gp_out.start()
    pair(gx_s, gx_r, 2).wait_recv()
    up_free.wait_recv()
    dn_free.wait_recv()
    up_last.wait_recv()
    dn_last.wait_recv()
    outs = [gq_out, gp_out]

    for ch in range(NCH):
        for which in (0, 1):
            for kind in range(4):
                ring(which, kind, ch).wait_send()
            hard_all(which, ch).wait_send()
        for n in range(1, 4):
            turn(0, n, ch).wait_send()
            turn(1, n, ch).wait_send()
    for dx in range(1, 4):
        x_peer(xt_s, xt_r, xt_send, xt_recv, dx).wait_send()
        x_peer(cx_s, cx_r, cx_send, cx_recv, dx).wait_send()
    for dz in range(1, 4):
        z_peer(dz).wait_send()
    yc_all(0).wait_send()
    yc_all(1).wait_send()
    pair(st_s, st_r, 0).wait_send()
    pair(lse_s, lse_r, 1).wait_send()
    pair(gx_s, gx_r, 2).wait_send()
    for copy in (far_up, far_dn, up_free, dn_free, up_last, dn_last):
        copy.wait_send()
    for copy in outs:
        copy.wait()


def results(loss_in, gq_in, gp_in, up_in, dn_in, gx_in, loss_out, gq_out, gp_out):
    loss_out[...] = loss_in[...]
    gq_out[...] = gq_in[...].astype(F32) + gx_in[...].astype(F32)
    gp_out[...] = gp_in[...].astype(F32) + up_in[...].astype(F32) + dn_in[...].astype(F32)


def on_device(ngrp, queries, passages, positives, hard_owner, hard_row):
    D = queries.shape[1]
    NC = 2 if ngrp % 4 == 0 else 1
    NY = ngrp // (2 * NC)
    R = 4 * NY * NC
    S = 16 * R
    shift = math.log(8 * ROWS / 3)
    vmem = pltpu.VMEM
    dma = pltpu.SemaphoreType.DMA
    wide = vmem((ROWS, D), BF16)
    parts = vmem((4, S // 4, D), BF16)
    any_spec = pl.BlockSpec(memory_space=pl.ANY)
    vmem_spec = pl.BlockSpec(memory_space=pltpu.VMEM)
    loss, gq, gp, up, dn, gx = pl.pallas_call(
        functools.partial(kernel, NY, NC, D, shift),
        out_shape=(
            jax.ShapeDtypeStruct((1, ROWS), F32),
            jax.ShapeDtypeStruct((ROWS, D), BF16),
            jax.ShapeDtypeStruct((ROWS, D), BF16),
            jax.ShapeDtypeStruct((ROWS, D), BF16),
            jax.ShapeDtypeStruct((ROWS, D), BF16),
            jax.ShapeDtypeStruct((ROWS, D), BF16),
        ),
        in_specs=[any_spec, any_spec, vmem_spec, vmem_spec, vmem_spec],
        out_specs=(vmem_spec,) + (any_spec,) * 5,
        scratch_shapes=[
            vmem((4 * ROWS, D), BF16), vmem((4 * ROWS, D), BF16),
            parts, parts, parts, parts, parts, parts,
            wide, wide, wide, wide, wide,
            vmem((ROWS, 4 * ROWS), F32), vmem((ROWS, 4 * ROWS), F32), vmem((ROWS, S), F32),
            vmem((2, S, 4 * ROWS), BF16),
            vmem((ROWS, 4 * ROWS), BF16), vmem((ROWS, 4 * ROWS), BF16), vmem((4 * ROWS, 2 * ROWS), BF16),
            vmem((ROWS, S), BF16),
            vmem((4, 4, S), F32), vmem((4, 4, S), F32),
            vmem((1, 1, S), F32), vmem((NY * NC, 1, S), F32),
            vmem((4, 1, S), F32), vmem((4, 1, S), F32),
            vmem((1, 2, S), F32), vmem((4, 2, S), F32),
            vmem((1, 2, S), F32), vmem((NY * NC, 2, S), F32),
            vmem((ROWS, 128), F32), vmem((ROWS, 128), F32), vmem((ROWS, 128), F32), vmem((ROWS, 128), F32),
            wide, wide,
            dma((2,)), dma((2,)), dma((2, 4, NCH)), dma((2, 4, NCH)), dma((2, NCH)), dma((2, NCH)),
            dma((4,)), dma((4,)), dma((4,)), dma((4,)), dma((4,)), dma((4,)), dma((2, 4, NCH)), dma((2, 4, NCH)), dma((2,)), dma((2,)), dma((3,)), dma((3,)),
            dma((6,)), dma((6,)),
        ],
        compiler_params=pltpu.CompilerParams(
            collective_id=0, has_side_effects=True, vmem_limit_bytes=60 * 2**20
        ),
        cost_estimate=pl.CostEstimate(flops=9 * 10**9, bytes_accessed=8 * 2**20, transcendentals=2 * 10**5),
        name="infonce",
    )(queries, passages, positives, hard_owner.T, hard_row.T)
    block = pl.BlockSpec((ROWS // 2, D), lambda i: (i, 0))
    row = pl.BlockSpec((1, ROWS), lambda i: (0, 0))
    loss, gq, gp = pl.pallas_call(
        results,
        grid=(2,),
        in_specs=[row, block, block, block, block, block],
        out_specs=(row, block, block),
        out_shape=tuple(jax.ShapeDtypeStruct(a.shape, F32) for a in (loss, gq, gp)),
        name="results",
    )(loss, gq, gp, up, dn, gx)
    return loss.reshape(ROWS), gq, gp


def solution(mesh):
    return jax.shard_map(
        functools.partial(on_device, mesh.shape["grp"]),
        mesh=mesh,
        in_specs=(
            P(("grp", "blk"), None),
            P(("grp", "blk"), None),
            P("grp", "blk"),
            P(("grp", "blk"), None),
            P(("grp", "blk"), None),
        ),
        out_specs=(P(("grp", "blk")), P(("grp", "blk"), None), P(("grp", "blk"), None)),
        check_vma=False,
    )
```
